512 devices in a mesh: lat: 128 (over x_hi, z, y), chan: 4 (over x_lo, core).
Axes of the slice: x: 4 (x_hi: 2, x_lo: 2; x = x_hi * 2 + x_lo), y: 4, z: 16, core: 2. Of those that a mesh axis runs over, the one named last changes fastest.
Arguments:
- input_field: bfloat16 [128, 384, 3072], P('lat', 'chan'), may hold values from -100 to 100
- cotangent: bfloat16 [128, 384, 3072], P('lat', 'chan'), may hold values from -6 to 6
- norm_gain: float32 [384], P('chan'), may hold values from 0.1 to 1.9
- inner_weights: bfloat16 [4, 2, 96, 96], P('chan'), may hold values from -0.4375 to 0.4375
- inner_bias: float32 [4, 2, 96], P('chan'), may hold values from -6 to 6
- outer_weights: bfloat16 [4, 2, 96, 96], P('chan'), may hold values from -0.4375 to 0.4375
- keep_codes: int32 [128, 1536, 384], P(None, 'lat', 'chan'), may hold values from 0 to 15
Outputs:
- grad_input: bfloat16 [128, 384, 3072], P('lat', 'chan')
- grad_inner_weights: float32 [4, 2, 96, 96], P('chan')
- grad_inner_bias: float32 [4, 2, 96], P('chan')
- grad_outer_weights: float32 [4, 2, 96, 96], P('chan')
- grad_outer_bias: float32 [4, 2, 96], P('chan')
- grad_gain: float32 [384], P('chan')
The draws below stay inside these ranges and needn't reach their ends.
Inputs may be any that keep to these rules, and one draw needn't show every extreme that they name: `keep_codes`: bits 0 and 1 belong to the hidden unit's real and imaginary part, bits 2 and 3 to the output channel's.
All inputs are finite; a program needn't handle non-finite values.
Results may differ from the reference program's by a relative error of at most 0.01.
Values may be sent and summed in bfloat16 or wider, within the bound.
A program may use at most 64 MiB of HBM per device.

```python
import math
import jax
import jax.numpy as jnp
from jax import lax

W = 3072
BS = 96
KW = 1536
NB = 4
C = 384
H = 128


def draw_input_field(key, part):
    key = jax.random.fold_in(key, 7)
    subkeys = jax.random.split(key, 4)
    channel_pos = jnp.arange(C).astype(jnp.float32) / (C - 1)
    channel_scale = jnp.exp(channel_pos * math.log(10.0) + jax.random.uniform(subkeys[0], (C,), minval=-0.3, maxval=0.3))
    channel_shift = jax.random.uniform(subkeys[1], (C,), minval=-1.0, maxval=1.0)
    cell_scale = jnp.exp(jax.random.uniform(subkeys[2], (H, 1, W), minval=0.0, maxval=math.log(10.0)))
    pattern = jnp.clip(jax.random.normal(subkeys[3], (H, C, W)), -4.0, 4.0)
    return (0.1 * cell_scale * channel_scale[None, :, None] * (pattern + channel_shift[None, :, None])).astype(jnp.bfloat16)


def place_ends(array, key, smallest, largest):
    index_at = [jax.random.randint(jax.random.fold_in(key, axis), (), 0, length) for axis, length in enumerate(array.shape)]
    main_axis = array.shape.index(max(array.shape))
    next_to = index_at[:main_axis] + [(index_at[main_axis] + 1) % array.shape[main_axis]] + index_at[main_axis + 1:]
    return array.at[tuple(index_at)].set(smallest).at[tuple(next_to)].set(largest)


def levels(own_key, extent, shards, low, largest):
    def one(axis_at, blocks):
        draws = jax.random.uniform(jax.random.fold_in(jax.random.fold_in(own_key, 6), axis_at), (blocks,), jnp.float32, low / len(shards), largest / len(shards))
        return jnp.repeat(jnp.exp(draws), extent[axis_at] // blocks).reshape((-1,) + (1,) * (len(extent) - axis_at - 1))

    factor_of = one(*shards[0])
    for cut in shards[1:]:
        factor_of = factor_of * one(*cut)
    return factor_of


def scatter_about(stream_key, dims, deviation, reach, pieces=(), kind=jnp.bfloat16):
    drawn = jax.random.normal(stream_key, dims, jnp.float32) * deviation
    if len(pieces) > 0:
        drawn = levels(stream_key, dims, pieces, -0.22, 0.18) * drawn
    return jnp.clip(drawn, min=-reach, max=reach).astype(kind)


def setup_inputs(seed: int = 0) -> dict:
    streams_of = jax.random.split(jax.random.key(seed), 8)
    input_field = draw_input_field(jax.random.fold_in(streams_of[7], 71), 0)
    cotangent = scatter_about(streams_of[1], (H, C, W), 1.0, 6.0, ((0, 128), (1, 4)))
    norm_gain = jnp.clip(1.0 + 0.18 * jax.random.normal(streams_of[2], (C,), jnp.float32), 0.1, 1.9)
    inner_weights = scatter_about(streams_of[3], (NB, 2, BS, BS), (2 * BS) ** -0.5, 0.4375, ((0, 4),))
    inner_bias = scatter_about(streams_of[4], (NB, 2, BS), 1.0, 6.0, ((0, 4),), jnp.float32)
    outer_weights = scatter_about(streams_of[5], (NB, 2, BS, BS), (2 * BS) ** -0.5, 0.4375, ((0, 4),))
    keep_codes = place_ends(jax.random.randint(streams_of[6], (H, KW, C), 0, 16), jax.random.fold_in(streams_of[6], 1), 0, 15).astype(jnp.int32)
    return dict(input_field=input_field, cotangent=cotangent, norm_gain=norm_gain, inner_weights=inner_weights, inner_bias=inner_bias, outer_weights=outer_weights, keep_codes=keep_codes)


def complex_matrix(weight_pair):
    real_part = weight_pair[0]
    imag_part = weight_pair[1]
    top_rows = jnp.concatenate([real_part, imag_part], axis=1)
    bottom_rows = jnp.concatenate([-imag_part, real_part], axis=1)
    return jnp.concatenate([top_rows, bottom_rows], axis=0)

def split_gradient(product, half_size):
    real_grad = product[:half_size, :half_size] + product[half_size:, half_size:]
    imag_grad = product[:half_size, half_size:] - product[half_size:, :half_size]
    return jnp.stack([real_grad, imag_grad])

def code_bit(code_rows, bit_place):
    return jnp.bitwise_and(jnp.right_shift(code_rows, bit_place), 1).astype(jnp.float32)

def rounded_parts(spectrum):
    return (spectrum.real.astype(jnp.bfloat16), spectrum.imag.astype(jnp.bfloat16))

def latitude_transform(real_part, imag_part, inverse):
    joined = real_part.astype(jnp.float32) + 1j * imag_part.astype(jnp.float32)
    if inverse:
        return jnp.fft.ifft(joined, axis=0, norm='ortho')
    return jnp.fft.fft(joined, axis=0, norm='ortho')

def reference(input_field, cotangent, norm_gain, inner_weights, inner_bias, outer_weights, keep_codes):
    block_ids = jnp.arange(NB, dtype=jnp.int32)

    def channel_block(source, block_id):
        return lax.dynamic_slice_in_dim(source, block_id * BS, BS, 1).astype(jnp.float32)

    def block_total(block_id):
        return lax.optimization_barrier(jnp.sum(channel_block(input_field, block_id), axis=1))
    centre = (lax.optimization_barrier(jnp.sum(lax.map(block_total, block_ids), axis=0)) / C)[:, None, :]

    def block_spread(block_id):
        offset = channel_block(input_field, block_id) - centre
        return lax.optimization_barrier(jnp.sum(offset * offset, axis=1))
    variance = lax.optimization_barrier(jnp.sum(lax.map(block_spread, block_ids), axis=0)) / C
    inv_std = (1.0 / jnp.sqrt(variance + 1e-05))[:, None, :]
    mode_ids = jnp.arange(KW)
    cot_weight = jnp.where(mode_ids == 0, 1.0, 2.0).astype(jnp.float32)
    back_weight = jnp.where(mode_ids == 0, 1.0, 0.5).astype(jnp.float32)
    grad_scale = 1.0 / math.sqrt(H * KW)
    gain_scale = 1.0 / math.sqrt(H * W)

    def block_pass(block_id):
        normed = (channel_block(input_field, block_id) - centre) * inv_std
        block_gain = lax.dynamic_slice_in_dim(norm_gain, block_id * BS, BS, 0).astype(jnp.float32)[None, :, None]
        spec_in = jnp.fft.rfft(normed * block_gain, axis=2, norm='ortho')[:, :, :KW]
        spec_cot = jnp.fft.rfft(channel_block(cotangent, block_id), axis=2, norm='ortho')[:, :, :KW] * cot_weight
        spec_real, spec_imag = rounded_parts(spec_in)
        in_real, in_imag = rounded_parts(latitude_transform(spec_real, spec_imag, False))
        freq_rows = jnp.concatenate([in_real, in_imag], axis=1).transpose(0, 2, 1).reshape(H * KW, 2 * BS)
        cot_real, cot_imag = rounded_parts(spec_cot)
        cot_freq = latitude_transform(cot_real, cot_imag, False)
        cot_rows = jnp.concatenate([cot_freq.real, cot_freq.imag], axis=1).transpose(0, 2, 1).reshape(H * KW, 2 * BS)
        code_rows = lax.dynamic_slice_in_dim(keep_codes, block_id * BS, BS, 2).reshape(H * KW, BS)
        relu_keep = jnp.concatenate([code_bit(code_rows, 0), code_bit(code_rows, 1)], axis=1)
        shrink_keep = jnp.concatenate([code_bit(code_rows, 2), code_bit(code_rows, 3)], axis=1)
        shrink_grad = (cot_rows * shrink_keep).astype(jnp.bfloat16)
        first_matrix = complex_matrix(inner_weights[block_id])
        second_matrix = complex_matrix(outer_weights[block_id])
        bias_row = inner_bias[block_id].reshape(2 * BS).astype(jnp.float32)
        hidden = ((jnp.dot(freq_rows, first_matrix, preferred_element_type=jnp.float32) + bias_row) * relu_keep).astype(jnp.bfloat16)
        outer_product = jnp.dot(hidden.T, shrink_grad, preferred_element_type=jnp.float32)
        back_hidden = (jnp.dot(shrink_grad, second_matrix.T, preferred_element_type=jnp.float32) * relu_keep).astype(jnp.bfloat16)
        inner_product = jnp.dot(freq_rows.T, back_hidden, preferred_element_type=jnp.float32)
        grad_rows = jnp.dot(back_hidden, first_matrix.T, preferred_element_type=jnp.float32)
        grad_freq = grad_rows.reshape(H, KW, 2 * BS).transpose(0, 2, 1)
        back_real, back_imag = rounded_parts(latitude_transform(grad_freq[:, :BS], grad_freq[:, BS:], True))
        joined = (back_real.astype(jnp.float32) + 1j * back_imag.astype(jnp.float32)) * back_weight
        padded = jnp.pad(joined, ((0, 0), (0, 0), (0, W // 2 + 1 - KW)))
        grad_norm = jnp.fft.irfft(padded, n=W, axis=2, norm='ortho')
        grad_hat = grad_norm * block_gain
        return (split_gradient(inner_product, BS) * grad_scale, lax.optimization_barrier(jnp.sum(back_hidden.astype(jnp.float32), axis=0)).reshape(2, BS) * grad_scale, split_gradient(outer_product, BS) * grad_scale, lax.optimization_barrier(jnp.sum(shrink_grad.astype(jnp.float32), axis=0)).reshape(2, BS) * grad_scale, lax.optimization_barrier(jnp.sum(grad_norm * normed, axis=(0, 2))) * gain_scale, grad_hat, lax.optimization_barrier(jnp.sum(grad_hat, axis=1)), lax.optimization_barrier(jnp.sum(grad_hat * normed, axis=1)))
    results = lax.map(block_pass, block_ids)
    inner_grad, inner_shift, outer_grad, outer_shift, gain_parts, grad_hats, hat_sums, cross_sums = results
    mean_hat = (lax.optimization_barrier(jnp.sum(hat_sums, axis=0)) / C)[:, None, :]
    mean_cross = (lax.optimization_barrier(jnp.sum(cross_sums, axis=0)) / C)[:, None, :]

    def finish(block_id):
        normed = (channel_block(input_field, block_id) - centre) * inv_std
        return ((grad_hats[block_id] - mean_hat - normed * mean_cross) * inv_std).astype(jnp.bfloat16)
    grad_blocks = lax.map(finish, block_ids)
    grad_input = jnp.transpose(grad_blocks, (1, 0, 2, 3)).reshape(H, C, W)
    return (grad_input, inner_grad, inner_shift, outer_grad, outer_shift, gain_parts.reshape(C))
```

```python
import math

import jax
import jax.numpy as jnp
import ml_dtypes
import numpy as np
from jax import lax
from jax.experimental import pallas as pl
from jax.experimental.pallas import tpu as pltpu
from jax.sharding import PartitionSpec as P

MESH = pl.DeviceIdType.MESH
BF = jnp.bfloat16
F32 = jnp.float32

LON = 3072
PT = 12
QT = 256
LAT = 128
CH = 96
ALL_CH = 384
NZ = 16
NJ = 8
CK = 3
MC = PT // CK
LC = MC * CH
LP = MC * 128
RW = 56
NP_ = RW // 8


def tables():
    z, p, j = np.meshgrid(np.arange(NZ), np.arange(2), np.arange(NJ), indexing="ij")
    dev = ((j // 4) * 64 + z * 4 + j % 4).reshape(-1)
    part = p.reshape(-1)
    q = np.arange(QT)
    ang = 2 * np.pi * ((dev[:, None] * q[None, :]) % QT) / QT
    cos, sin = np.cos(ang), np.sin(ang)
    re = part[:, None] == 0
    fwd = np.concatenate([np.where(re, cos, -sin), np.where(re, sin, cos)], 1) / math.sqrt(LON)
    inv = np.concatenate([np.where(re, cos, -sin), np.where(re, sin, cos)], 1) / math.sqrt(LON)
    j2, p2, z2 = np.meshgrid(np.arange(NJ), np.arange(2), np.arange(NZ), indexing="ij")
    dev2 = ((j2 // 4) * 64 + z2 * 4 + j2 % 4).reshape(-1)
    part2 = p2.reshape(-1)
    mode = np.arange(LAT)
    ang2 = 2 * np.pi * ((mode[:, None] * dev2[None, :]) % LAT) / LAT
    c2, s2 = np.cos(ang2), np.sin(ang2)
    re2 = part2[None, :] == 0
    lat = np.concatenate([np.where(re2, c2, s2), np.where(re2, -s2, c2)], 0) / math.sqrt(LAT)
    pos = (z2 * 2 * NJ + p2 * NJ + j2).reshape(-1)
    perm = np.zeros((256, 256))
    perm[np.arange(256), pos] = 1.0
    widen = np.zeros((LC, LP))
    for i in range(MC):
        widen[i * CH + np.arange(CH), i * 128 + np.arange(CH)] = 1.0
    turn = 2 * np.pi * np.arange(PT)[:, None] * q[None, :] / LON
    twiddle = np.concatenate([np.cos(turn), np.sin(turn)], 0)
    bf = [a.astype(ml_dtypes.bfloat16) for a in (fwd, inv, lat, lat.T, perm, perm.T, widen, widen.T)]
    return bf + [twiddle.astype(np.float32)]


def real12(u0, u6, s, t):
    h = 0.5
    r3 = math.sqrt(3.0) / 2
    ap, am = u0 + u6, u0 - u6
    s24, d24 = s[2] + s[4], s[2] - s[4]
    s15, d15 = s[1] + s[5], s[1] - s[5]
    e0, o0 = ap + s24, s15 + s[3]
    e1, o1 = am + h * d24, r3 * d15
    e2, o2 = ap - h * s24, h * s15 - s[3]
    real = [e0 + o0, e1 + o1, e2 + o2, am - d24, e2 - o2, e1 - o1, e0 - o0]
    t15, f15 = t[1] + t[5], t[1] - t[5]
    t24, f24 = t[2] + t[4], t[2] - t[4]
    a1, b1 = h * t15 + t[3], r3 * t24
    a2, b2 = r3 * f15, r3 * f24
    imag = [None, -(a1 + b1), -(a2 + b2), t[3] - t15, b2 - a2, b1 - a1, None]
    return real, imag


def dot_nn(a, b):
    return lax.dot_general(a, b, (((1,), (0,)), ((), ())), preferred_element_type=F32)


def dot_nt(a, b):
    return lax.dot_general(a, b, (((1,), (1,)), ((), ())), preferred_element_type=F32)


def dot_tn(a, b):
    return lax.dot_general(a, b, (((0,), (0,)), ((), ())), preferred_element_type=F32)


def kernel(
    x_ref, cot_ref, gain_ref, iw_ref, ib_ref, ow_ref, code_ref,
    fwd_ref, inv_ref, lat_ref, lati_ref, perm_ref, permi_ref, wide_ref, narrow_ref, tw_ref,
    gin_ref, giw_ref, gib_ref, gow_ref, gob_ref, gg_ref,
    ybuf, zs, zr, xs, xr, bxs, bxr, bzs, bzr,
    stat_s, stat_r, tail_s, tail_r, mr, gcol,
    m1, m2, bias, cm, sg_all, bh_all, fi, hd, gp, p1, p2, bsum,
    vbuf, gbuf, hacc, cacc,
    rw, rr1, rs, rr2, rt, rr2b, rr3,
    zs_sem, zr_sem, xs_sem, xr_sem, bxs_sem, bxr_sem, bzs_sem, bzr_sem,
    st_ssem, st_rsem, tl_ssem, tl_rsem,
    r1_ssem, r1_rsem, r2_ssem, r2_rsem, r2b_ssem, r2b_rsem, r3_ssem, r3_rsem,
):
    me = lax.axis_index("lat")
    chan = lax.axis_index("chan")
    x = me // 64
    z = lax.rem(me // 4, NZ)
    y = lax.rem(me, 4)
    j = x * 4 + y
    base_z = me - z * 4

    def z_step(t):
        half = t // 2
        odd = lax.rem(t, 2)
        off = (half + 1) * (1 - odd) + (NZ - 1 - half) * odd
        to = lax.rem(z + off, NZ)
        return to, {"lat": base_z + to * 4}

    def xy_step(t):
        d = t + 1
        tx = lax.rem(x + d // 4, 2)
        ty = lax.rem(y + lax.rem(d, 4), 4)
        return tx * 4 + ty, {"lat": tx * 64 + z * 4 + ty}

    def chan_step(t):
        to = lax.rem(chan + t + 1, 4)
        return to, {"chan": to}

    def each(count, body):
        def one(t, carry):
            body(t)
            return carry

        lax.fori_loop(0, count, one, 0)

    def remote(src, dst, ssem, rsem, to):
        pltpu.make_async_remote_copy(
            src_ref=src, dst_ref=dst, send_sem=ssem, recv_sem=rsem, device_id=to, device_id_type=MESH
        ).start()

    def drain(ref, sem):
        pltpu.make_async_copy(ref, ref, sem).wait()

    def z_exchange(src, dst, ssem, rsem):
        def send(t):
            to, dev = z_step(t)
            remote(src.at[to], dst.at[z], ssem, rsem, dev)

        each(NZ - 1, send)
        dst[z] = src[z]

    def xy_exchange(src, dst, ssem, rsem):
        def send(t):
            to, dev = xy_step(t)
            remote(src.at[to], dst.at[j], ssem, rsem, dev)

        each(NJ - 1, send)
        dst[j] = src[j]

    def xy_share(src, dst, ssem, rsem):
        def send(t):
            _, dev = xy_step(t)
            remote(src, dst.at[j], ssem, rsem, dev)

        each(NJ - 1, send)
        dst[j] = src[...]

    def chan_share(src, dst, ssem, rsem):
        def send(t):
            _, dev = chan_step(t)
            remote(src, dst.at[chan], ssem, rsem, dev)

        each(3, send)
        dst[chan] = src[...]

    def z_done(ref, sem):
        drain(ref.at[pl.ds(0, NZ - 1)], sem)

    def xy_done(ref, sem):
        drain(ref.at[pl.ds(0, NJ - 1)], sem)

    barrier = pltpu.get_barrier_semaphore()

    def greet(step):
        def one(t):
            _, dev = step(t)
            pl.semaphore_signal(barrier, inc=1, device_id=dev, device_id_type=MESH)

        return one

    each(NZ - 1, greet(z_step))
    each(NJ - 1, greet(xy_step))
    each(3, greet(chan_step))

    def lanes(p):
        return slice(p * QT, (p + 1) * QT)

    def forward_rows(load):
        def block(r):
            r0 = pl.multiple_of(r * 16, 16)
            u = [load(r0, p) for p in range(PT)]
            s = [None] + [u[p] + u[PT - p] for p in range(1, 6)]
            t = [None] + [u[p] - u[PT - p] for p in range(1, 6)]
            real, imag = real12(u[0], u[6], s, t)
            for i in range(PT):
                k = i if i <= 6 else PT - i
                yr = real[k]
                yi = imag[k]
                c = tw_ref[i : i + 1, :]
                w = tw_ref[PT + i : PT + i + 1, :]
                if yi is None:
                    ar, ai = yr * c, -(yr * w)
                elif i <= 6:
                    ar, ai = yr * c + yi * w, yi * c - yr * w
                else:
                    ar, ai = yr * c - yi * w, -(yi * c) - yr * w
                rows = pl.ds(pl.multiple_of(i * CH + r0, 16), 16)
                ybuf[rows, 0:QT] = ar.astype(BF)
                ybuf[rows, QT : 2 * QT] = ai.astype(BF)

        each(CH // 16, block)

    def dft_chunk(c):
        return dot_nt(fwd_ref[...], ybuf[pl.ds(c * LC, LC), :])

    forward_rows(lambda r0, p: cot_ref[0, pl.ds(r0, 16), lanes(p)].astype(F32) * 2.0)
    for c in range(CK):
        out = dft_chunk(c)
        if c == 0:
            row = lax.broadcasted_iota(jnp.int32, out.shape, 0)
            lane = lax.broadcasted_iota(jnp.int32, out.shape, 1)
            first = ((row == 0) | (row == NJ)) & (lane < CH)
            out = out * jnp.where(first, 0.5, 1.0)
        zs[0, c] = out.astype(BF).reshape(NZ, 16, LC)
        if c == 0:
            pl.semaphore_wait(barrier, NZ - 1 + NJ - 1 + 3)
        z_exchange(zs.at[0, c], zr.at[0, c], zs_sem.at[0, c], zr_sem.at[0, c])

    for p in range(PT):
        v = x_ref[0, :, lanes(p)].astype(F32)
        total = jnp.sum(v, axis=0, keepdims=True)
        off = v - total * (1.0 / CH)
        r, l = p // 3, (p % 3) * QT
        stat_s[r : r + 1, l : l + QT] = total
        stat_s[4 + r : 5 + r, l : l + QT] = jnp.sum(off * off, axis=0, keepdims=True)
    chan_share(stat_s, stat_r, st_ssem, st_rsem)

    diag = (
        lax.broadcasted_iota(jnp.int32, (CH, CH), 0) == lax.broadcasted_iota(jnp.int32, (CH, CH), 1)
    ).astype(F32)
    gcol[...] = jnp.sum(diag * gain_ref[...], axis=1, keepdims=True)
    for m, w in ((m1, iw_ref), (m2, ow_ref)):
        m[...] = jnp.zeros(m.shape, BF)
        m[0:CH, 0:CH] = w[0, 0]
        m[0:CH, 128 : 128 + CH] = w[0, 1]
        m[128 : 128 + CH, 0:CH] = -w[0, 1]
        m[128 : 128 + CH, 128 : 128 + CH] = w[0, 0]
    bias[...] = jnp.zeros(bias.shape, F32)
    bias[0:1, 0:CH] = ib_ref[0, 0:1, :]
    bias[0:1, 128 : 128 + CH] = ib_ref[0, 1:2, :]
    cm[...] = jnp.zeros(cm.shape, jnp.int32)
    for i in range(PT):
        cm[i, :, 0:CH] = code_ref[:, i, :]
    p1[...] = jnp.zeros(p1.shape, F32)
    p2[...] = jnp.zeros(p2.shape, F32)
    bsum[...] = jnp.zeros(bsum.shape, F32)

    drain(stat_r.at[pl.ds(0, 3)], st_rsem)
    for p in range(PT):
        r, l = p // 3, (p % 3) * QT
        sums = [stat_r[d, r : r + 1, l : l + QT] for d in range(4)]
        spreads = [stat_r[d, 4 + r : 5 + r, l : l + QT] for d in range(4)]
        mean = (sums[0] + sums[1] + sums[2] + sums[3]) * (1.0 / ALL_CH)
        spread = spreads[0] + spreads[1] + spreads[2] + spreads[3]
        for d in range(4):
            gap = sums[d] * (1.0 / CH) - mean
            spread = spread + CH * gap * gap
        mr[0:1, lanes(p)] = mean
        mr[1:2, lanes(p)] = lax.rsqrt(spread * (1.0 / ALL_CH) + 1e-05)

    def xhat(r0, p):
        v = x_ref[0, pl.ds(r0, 16), lanes(p)].astype(F32)
        return (v - mr[0:1, lanes(p)]) * mr[1:2, lanes(p)]

    forward_rows(lambda r0, p: xhat(r0, p) * gcol[pl.ds(r0, 16), :])
    for c in range(CK):
        zs[1, c] = dft_chunk(c).astype(BF).reshape(NZ, 16, LC)
        z_exchange(zs.at[1, c], zr.at[1, c], zs_sem.at[1, c], zr_sem.at[1, c])

    def second_exchange(f, c):
        z_done(zr.at[f, c], zr_sem.at[f, c])
        got = zr[f, c].reshape(256, LC)
        xs[f, c] = dot_nn(perm_ref[...], got).astype(BF).reshape(NJ, 32, LC)
        xy_exchange(xs.at[f, c], xr.at[f, c], xs_sem.at[f, c], xr_sem.at[f, c])

    def latitude_modes(f, c):
        xy_done(xr.at[f, c], xr_sem.at[f, c])
        spread = dot_nn(xr[f, c].reshape(256, LC), wide_ref[...]).astype(BF)
        return dot_nn(lat_ref[...], spread)

    def bit(code, place):
        return jnp.bitwise_and(jnp.right_shift(code, place), 1).astype(F32)

    def mode_rows(c, i):
        return slice((c * MC + i) * 128, (c * MC + i + 1) * 128)

    def masked(dst, rows, value, code, place):
        dst[rows, 0:128] = (value[0] * bit(code, place)).astype(BF)
        dst[rows, 128:256] = (value[1] * bit(code, place + 1)).astype(BF)

    def backward_chunk(c):
        freq = latitude_modes(0, c)
        for i in range(MC):
            col = slice(i * 128, (i + 1) * 128)
            masked(sg_all, mode_rows(c, i), (freq[0:128, col], freq[128:256, col]), cm[c * MC + i], 2)
        chunk = slice(c * LP, (c + 1) * LP)
        back = dot_nt(sg_all[chunk, :], m2[...])
        for i in range(MC):
            row = slice(i * 128, (i + 1) * 128)
            masked(bh_all, mode_rows(c, i), (back[row, 0:128], back[row, 128:256]), cm[c * MC + i], 0)
        grad = dot_nt(bh_all[chunk, :], m1[...]).astype(BF)
        for i in range(MC):
            row = slice(i * 128, (i + 1) * 128)
            gp[0:128, row] = grad[row, 0:128]
            gp[128:256, row] = grad[row, 128:256]
        spec = dot_nn(lati_ref[...], gp[...]).astype(BF)
        bxs[c] = dot_nn(spec, narrow_ref[...]).astype(BF).reshape(NJ, 32, LC)
        xy_exchange(bxs.at[c], bxr.at[c], bxs_sem.at[c], bxr_sem.at[c])

    def second_back(c):
        xy_done(bxr.at[c], bxr_sem.at[c])
        got = bxr[c].reshape(256, LC)
        bzs[c] = dot_nn(permi_ref[...], got).astype(BF).reshape(NZ, 16, LC)
        z_exchange(bzs.at[c], bzr.at[c], bzs_sem.at[c], bzr_sem.at[c])

    def weight_chunk(c):
        freq = latitude_modes(1, c)
        for i in range(MC):
            row = slice(i * 128, (i + 1) * 128)
            fi[row, 0:128] = freq[0:128, row].astype(BF)
            fi[row, 128:256] = freq[128:256, row].astype(BF)
        pre = dot_nn(fi[...], m1[...]) + bias[0:1, :]
        for i in range(MC):
            row = slice(i * 128, (i + 1) * 128)
            masked(hd, row, (pre[row, 0:128], pre[row, 128:256]), cm[c * MC + i], 0)
        chunk = slice(c * LP, (c + 1) * LP)
        sg, bh = sg_all[chunk, :], bh_all[chunk, :]
        p2[...] += dot_tn(hd[...], sg)
        p1[...] += dot_tn(fi[...], bh)
        bsum[0:1, :] += jnp.sum(bh.astype(F32), axis=0, keepdims=True)
        bsum[1:2, :] += jnp.sum(sg.astype(F32), axis=0, keepdims=True)

    second_exchange(0, 0)
    second_exchange(0, 1)
    backward_chunk(0)
    second_exchange(0, 2)
    backward_chunk(1)
    second_back(0)
    backward_chunk(2)
    second_back(1)
    second_exchange(1, 0)
    second_back(2)
    second_exchange(1, 1)
    weight_chunk(0)
    second_exchange(1, 2)
    weight_chunk(1)
    weight_chunk(2)

    for s, src in ((0, p1), (4, p2)):
        real = src[0:CH, 0:128] + src[128 : 128 + CH, 128:256]
        imag = src[0:CH, 128:256] - src[128 : 128 + CH, 0:128]
        rw[s, 0:48] = real[0:48]
        rw[s + 1, 0:48] = real[48:96]
        rw[s + 2, 0:48] = imag[0:48]
        rw[s + 3, 0:48] = imag[48:96]
    for s in range(NJ):
        rw[s, 48:56] = jnp.zeros((8, 128), F32)
    rw[0, 48:49] = bsum[0:1, 0:128]
    rw[0, 49:50] = bsum[0:1, 128:256]
    rw[0, 50:51] = bsum[1:2, 0:128]
    rw[0, 51:52] = bsum[1:2, 128:256]
    xy_exchange(rw, rr1, r1_ssem, r1_rsem)

    def inverse_chunk(c):
        z_done(bzr.at[c], bzr_sem.at[c])
        got = bzr[c].reshape(256, LC)
        vbuf[pl.ds(c * LC, LC), :] = dot_tn(got, inv_ref[...])

    inverse_chunk(0)

    xy_done(rr1, r1_rsem)
    part = rr1[0]
    for s in range(1, NJ):
        part = part + rr1[s]
    rs[...] = part.reshape(NP_, 8, 128)
    owner = (lax.rem(z, 2) == 0) & (z < 2 * NP_)
    piece = z // 2
    for t in range(NP_):
        @pl.when(z != 2 * t)
        def _():
            remote(rs.at[t], rr2.at[z], r2_ssem, r2_rsem, {"lat": base_z + 8 * t})

    @pl.when(owner)
    def _():
        rr2[z] = rs[piece]
        z_done(rr2, r2_rsem)
        total = rr2[0]
        for s in range(1, NZ):
            total = total + rr2[s]
        rt[...] = total
        rr2b[piece] = total

        def send(t):
            _, dev = z_step(t)
            remote(rt, rr2b.at[piece], r2b_ssem, r2b_rsem, dev)

        each(NZ - 1, send)

    inverse_chunk(1)

    @pl.when(owner)
    def _():
        drain(rr2b.at[pl.ds(0, NP_ - 1)], r2b_rsem)

    @pl.when(jnp.logical_not(owner))
    def _():
        drain(rr2b, r2b_rsem)

    xy_share(rr2b, rr3, r3_ssem, r3_rsem)

    inverse_chunk(2)

    hacc[...] = jnp.zeros(hacc.shape, F32)
    cacc[...] = jnp.zeros(cacc.shape, F32)

    def inverse_rows(r):
        r0 = pl.multiple_of(r * 16, 16)
        re, im = [], []
        for i in range(PT):
            rows = pl.ds(pl.multiple_of(i * CH + r0, 16), 16)
            vr = vbuf[rows, 0:QT]
            vi = vbuf[rows, QT : 2 * QT]
            c = tw_ref[i : i + 1, :]
            w = tw_ref[PT + i : PT + i + 1, :]
            re.append(vr * c - vi * w)
            im.append(None if i in (0, 6) else vr * w + vi * c)
        s = [None] + [re[i] + re[PT - i] for i in range(1, 6)]
        t = [None] + [im[i] - im[PT - i] for i in range(1, 6)]
        real, imag = real12(re[0], re[6], s, t)
        column = gcol[pl.ds(r0, 16), :]
        for p in range(PT):
            k = p if p <= 6 else PT - p
            v = real[k]
            if imag[k] is not None:
                v = v + imag[k] if p <= 6 else v - imag[k]
            v = v * column
            gbuf[pl.ds(r0, 16), lanes(p)] = v
            hacc[:, lanes(p)] += v
            cacc[:, lanes(p)] += v * xhat(r0, p)

    each(CH // 16, inverse_rows)
    for p in range(PT):
        r, l = p // 3, (p % 3) * QT
        tail_s[r : r + 1, l : l + QT] = jnp.sum(hacc[:, lanes(p)], axis=0, keepdims=True)
        tail_s[4 + r : 5 + r, l : l + QT] = jnp.sum(cacc[:, lanes(p)], axis=0, keepdims=True)
    chan_share(tail_s, tail_r, tl_ssem, tl_rsem)

    xy_done(rr3, r3_rsem)
    scale = 1.0 / math.sqrt(LAT * LON / 2)

    def summed(s):
        return rr3[s, 0:6].reshape(48, 128)[:, 0:CH]

    for s, out in ((0, giw_ref), (4, gow_ref)):
        for k in range(2):
            out[0, k, 0:48] = summed(s + 2 * k) * scale
            out[0, k, 48:96] = summed(s + 2 * k + 1) * scale
    gib_ref[0, 0:2] = rr3[0, 6, 0:2, 0:CH] * scale
    gob_ref[0, 0:2] = rr3[0, 6, 2:4, 0:CH] * scale
    product = jnp.zeros((CH, CH), F32)
    for k in range(2):
        whole = jnp.concatenate([summed(2 * k), summed(2 * k + 1)], axis=0)
        product = product + whole * iw_ref[0, k].astype(F32)
    column = jnp.sum(product, axis=1, keepdims=True)
    as_row = jnp.sum(diag * column, axis=0, keepdims=True)
    gg_ref[...] = as_row * (1.0 / math.sqrt(LAT * LON)) / gain_ref[...]

    drain(tail_r.at[pl.ds(0, 3)], tl_rsem)
    for p in range(PT):
        r, l = p // 3, (p % 3) * QT
        for k in range(2):
            q = 4 * k + r
            total = tail_r[0, q : q + 1, l : l + QT]
            for d in range(1, 4):
                total = total + tail_r[d, q : q + 1, l : l + QT]
            mr[2 + k : 3 + k, lanes(p)] = total * (1.0 / ALL_CH)

    def finish_rows(r):
        r0 = pl.multiple_of(r * 16, 16)
        for p in range(PT):
            g = gbuf[pl.ds(r0, 16), lanes(p)]
            v = g - mr[2:3, lanes(p)] - xhat(r0, p) * mr[3:4, lanes(p)]
            gin_ref[0, pl.ds(r0, 16), lanes(p)] = (v * mr[1:2, lanes(p)]).astype(BF)

    each(CH // 16, finish_rows)

    for c in range(CK):
        for f in range(2):
            z_done(zs.at[f, c], zs_sem.at[f, c])
            xy_done(xs.at[f, c], xs_sem.at[f, c])
        xy_done(bxs.at[c], bxs_sem.at[c])
        z_done(bzs.at[c], bzs_sem.at[c])
    drain(stat_r.at[pl.ds(0, 3)], st_ssem)
    drain(tail_r.at[pl.ds(0, 3)], tl_ssem)
    xy_done(rw, r1_ssem)
    xy_done(rr3, r3_ssem)

    @pl.when(owner)
    def _():
        drain(rs.at[pl.ds(0, NP_ - 1)], r2_ssem)
        z_done(rr2, r2b_ssem)

    @pl.when(jnp.logical_not(owner))
    def _():
        drain(rs, r2_ssem)


def per_device(field, cot, gain, inner_w, inner_b, outer_w, codes):
    vm = pl.BlockSpec(memory_space=pltpu.VMEM)
    tabs = [jnp.asarray(t) for t in tables()]
    S = jax.ShapeDtypeStruct
    dma = pltpu.SemaphoreType.DMA
    V = pltpu.VMEM
    scratch = [
        V((PT * CH, 2 * QT), BF),
        V((2, CK, NZ, 16, LC), BF), V((2, CK, NZ, 16, LC), BF),
        V((2, CK, NJ, 32, LC), BF), V((2, CK, NJ, 32, LC), BF),
        V((CK, NJ, 32, LC), BF), V((CK, NJ, 32, LC), BF),
        V((CK, NZ, 16, LC), BF), V((CK, NZ, 16, LC), BF),
        V((8, 768), F32), V((4, 8, 768), F32), V((8, 768), F32), V((4, 8, 768), F32),
        V((8, LON), F32), V((CH, 1), F32),
        V((256, 256), BF), V((256, 256), BF), V((8, 256), F32), V((PT, 128, 128), jnp.int32),
        V((PT * 128, 256), BF), V((PT * 128, 256), BF), V((LP, 256), BF), V((LP, 256), BF),
        V((256, LP), BF), V((256, 256), F32), V((256, 256), F32), V((8, 256), F32),
        V((PT * CH, 2 * QT), F32), V((CH, LON), F32), V((16, LON), F32), V((16, LON), F32),
        V((NJ, RW, 128), F32), V((NJ, RW, 128), F32), V((NP_, 8, 128), F32), V((NZ, 8, 128), F32),
        V((8, 128), F32), V((NP_, 8, 128), F32), V((NJ, NP_, 8, 128), F32),
        dma((2, CK)), dma((2, CK)), dma((2, CK)), dma((2, CK)),
        dma((CK,)), dma((CK,)), dma((CK,)), dma((CK,)),
    ] + [dma(())] * 12
    outs = pl.pallas_call(
        kernel,
        out_shape=(
            S((1, CH, LON), BF),
            S((1, 2, CH, CH), F32),
            S((1, 2, CH), F32),
            S((1, 2, CH, CH), F32),
            S((1, 2, CH), F32),
            S((1, CH), F32),
        ),
        in_specs=[vm] * 16,
        out_specs=(vm,) * 6,
        scratch_shapes=scratch,
        compiler_params=pltpu.CompilerParams(
            collective_id=0, has_side_effects=True, vmem_limit_bytes=56 * 2**20
        ),
        name="mixing_backward",
    )(field, cot, gain.reshape(1, CH), inner_w, inner_b, outer_w, codes, *tabs)
    return outs[:5] + (outs[5].reshape(CH),)


def solution(mesh):
    in_specs = (
        P("lat", "chan", None),
        P("lat", "chan", None),
        P("chan"),
        P("chan", None, None, None),
        P("chan", None, None),
        P("chan", None, None, None),
        P(None, "lat", "chan"),
    )
    out_specs = (
        P("lat", "chan", None),
        P("chan", None, None, None),
        P("chan", None, None),
        P("chan", None, None, None),
        P("chan", None, None),
        P("chan"),
    )
    return jax.shard_map(
        per_device, mesh=mesh, in_specs=in_specs, out_specs=out_specs, check_vma=False
    )
```

```python
import math

import jax
import jax.numpy as jnp
import ml_dtypes
import numpy as np
from jax import lax
from jax.experimental import pallas as pl
from jax.experimental.pallas import tpu as pltpu
from jax.sharding import PartitionSpec as P

MESH = pl.DeviceIdType.MESH
BF = jnp.bfloat16
F32 = jnp.float32

LON = 3072
PT = 12
QT = 256
LAT = 128
CH = 96
ALL_CH = 384
NZ = 16
NJ = 8
CK = 3
MC = PT // CK
LC = MC * CH
LP = MC * 128
RW = 64
FR = 48
NEAR = 4
RP = RW // NEAR


def tables():
    z, p, j = np.meshgrid(np.arange(NZ), np.arange(2), np.arange(NJ), indexing="ij")
    dev = ((j // 4) * 64 + z * 4 + j % 4).reshape(-1)
    part = p.reshape(-1)
    q = np.arange(QT)
    ang = 2 * np.pi * ((dev[:, None] * q[None, :]) % QT) / QT
    cos, sin = np.cos(ang), np.sin(ang)
    re = part[:, None] == 0
    fwd = np.concatenate([np.where(re, cos, -sin), np.where(re, sin, cos)], 1) / math.sqrt(LON)
    inv = np.concatenate([np.where(re, cos, -sin), np.where(re, sin, cos)], 1) / math.sqrt(LON)
    j2, p2, z2 = np.meshgrid(np.arange(NJ), np.arange(2), np.arange(NZ), indexing="ij")
    dev2 = ((j2 // 4) * 64 + z2 * 4 + j2 % 4).reshape(-1)
    part2 = p2.reshape(-1)
    mode = np.arange(LAT)
    ang2 = 2 * np.pi * ((mode[:, None] * dev2[None, :]) % LAT) / LAT
    c2, s2 = np.cos(ang2), np.sin(ang2)
    re2 = part2[None, :] == 0
    lat = np.concatenate([np.where(re2, c2, s2), np.where(re2, -s2, c2)], 0) / math.sqrt(LAT)
    pos = (z2 * 2 * NJ + p2 * NJ + j2).reshape(-1)
    perm = np.zeros((256, 256))
    perm[np.arange(256), pos] = 1.0
    widen = np.zeros((LC, LP))
    for i in range(MC):
        widen[i * CH + np.arange(CH), i * 128 + np.arange(CH)] = 1.0
    turn = 2 * np.pi * np.arange(PT)[:, None] * q[None, :] / LON
    twiddle = np.concatenate([np.cos(turn), np.sin(turn)], 0)
    order = (fwd, perm @ fwd, inv, lat, lat @ perm, lat.T, perm, perm.T, widen, widen.T)
    bf = [a.astype(ml_dtypes.bfloat16) for a in order]
    return bf + [twiddle.astype(np.float32)]


def real12(u0, u6, s, t):
    h = 0.5
    r3 = math.sqrt(3.0) / 2
    ap, am = u0 + u6, u0 - u6
    s24, d24 = s[2] + s[4], s[2] - s[4]
    s15, d15 = s[1] + s[5], s[1] - s[5]
    e0, o0 = ap + s24, s15 + s[3]
    e1, o1 = am + h * d24, r3 * d15
    e2, o2 = ap - h * s24, h * s15 - s[3]
    real = [e0 + o0, e1 + o1, e2 + o2, am - d24, e2 - o2, e1 - o1, e0 - o0]
    t15, f15 = t[1] + t[5], t[1] - t[5]
    t24, f24 = t[2] + t[4], t[2] - t[4]
    a1, b1 = h * t15 + t[3], r3 * t24
    a2, b2 = r3 * f15, r3 * f24
    imag = [None, -(a1 + b1), -(a2 + b2), t[3] - t15, b2 - a2, b1 - a1, None]
    return real, imag


def dot_nn(a, b):
    return lax.dot_general(a, b, (((1,), (0,)), ((), ())), preferred_element_type=F32)


def dot_nt(a, b):
    return lax.dot_general(a, b, (((1,), (1,)), ((), ())), preferred_element_type=F32)


def dot_tn(a, b):
    return lax.dot_general(a, b, (((0,), (0,)), ((), ())), preferred_element_type=F32)


def kernel(
    x_hbm, cot_hbm, code_hbm, fwd_hbm, fwdx_hbm, inv_hbm, lat_hbm, latz_hbm, lati_hbm,
    perm_hbm, permi_hbm, wide_hbm, narrow_hbm,
    gain_ref, iw_ref, ib_ref, ow_ref, tw_ref,
    g_ref, cell_ref, wout_ref, bout_ref,
    x_ref, cot_ref, code_ref, fwd_ref, fwdx_ref, inv_ref, lat_ref, latz_ref, lati_ref,
    perm_ref, permi_ref, wide_ref, narrow_ref, load_sem,
    ybuf, zs, zr, xs, xr, bxs, bxr, bzs, bzr,
    stat_s, stat_r, tail_s, tail_r, mr, gcol,
    m1, m2, bias, cm, sg_all, bh_all, fi, hd, gp, p1, p2, bsum,
    vbuf, hacc, cacc,
    rw, rr1, rs, rr2, rt, rr3, ru, rr4, rv, rr5,
    zs_sem, zr_sem, xs_sem, xr_sem, bxs_sem, bxr_sem, bzs_sem, bzr_sem,
    st_ssem, st_rsem, tl_ssem, tl_rsem,
    r1_ssem, r1_rsem, r2_ssem, r2_rsem, r3_ssem, r3_rsem, r4_ssem, r4_rsem, r5_ssem, r5_rsem,
):
    me = lax.axis_index("lat")
    chan = lax.axis_index("chan")
    x = me // 64
    z = lax.rem(me // 4, NZ)
    y = lax.rem(me, 4)
    j = x * 4 + y
    base_z = me - z * 4

    def z_step(t):
        half = t // 2
        odd = lax.rem(t, 2)
        off = (half + 1) * (1 - odd) + (NZ - 1 - half) * odd
        to = lax.rem(z + off, NZ)
        return to, {"lat": base_z + to * 4}

    def xy_step(t):
        d = t + 1
        tx = lax.rem(x + d // 4, 2)
        ty = lax.rem(y + lax.rem(d, 4), 4)
        return tx * 4 + ty, {"lat": tx * 64 + z * 4 + ty}

    near, block = lax.rem(z, NEAR), z // NEAR

    def near_step(t):
        to = lax.rem(near + t + 1, NEAR)
        return to, {"lat": base_z + (block * NEAR + to) * 4}

    def far_step(t):
        to = lax.rem(block + t + 1, NZ // NEAR)
        return to, {"lat": base_z + (to * NEAR + near) * 4}

    def chan_step(t):
        to = lax.rem(chan + t + 1, 4)
        return to, {"chan": to}

    def each(count, body):
        def one(t, carry):
            body(t)
            return carry

        lax.fori_loop(0, count, one, 0)

    def remote(src, dst, ssem, rsem, to):
        pltpu.make_async_remote_copy(
            src_ref=src, dst_ref=dst, send_sem=ssem, recv_sem=rsem, device_id=to, device_id_type=MESH
        ).start()

    def drain(ref, sem):
        pltpu.make_async_copy(ref, ref, sem).wait()

    def z_exchange(src, dst, ssem, rsem):
        def send(t):
            to, dev = z_step(t)
            remote(src.at[to], dst.at[z], ssem, rsem, dev)

        each(NZ - 1, send)
        dst[z] = src[z]

    def xy_exchange(src, dst, ssem, rsem):
        def send(t):
            to, dev = xy_step(t)
            remote(src.at[to], dst.at[j], ssem, rsem, dev)

        each(NJ - 1, send)
        dst[j] = src[j]

    def share(step, count, place, src, dst, ssem, rsem):
        def send(t):
            _, dev = step(t)
            remote(src, dst.at[place], ssem, rsem, dev)

        each(count - 1, send)
        dst[place] = src[...]

    def chan_share(src, dst, ssem, rsem):
        share(chan_step, 4, chan, src, dst, ssem, rsem)

    def rest(ref, count, sem):
        drain(ref.at[pl.ds(0, count - 1)], sem)

    def z_done(ref, sem):
        drain(ref.at[pl.ds(0, NZ - 1)], sem)

    def xy_done(ref, sem):
        drain(ref.at[pl.ds(0, NJ - 1)], sem)

    barrier = pltpu.get_barrier_semaphore()

    def greet(step):
        def one(t):
            _, dev = step(t)
            pl.semaphore_signal(barrier, inc=1, device_id=dev, device_id_type=MESH)

        return one

    each(NZ - 1, greet(z_step))
    each(NJ - 1, greet(xy_step))
    each(3, greet(chan_step))

    loads = [
        pltpu.make_async_copy(src, dst, load_sem.at[k])
        for k, (src, dst) in enumerate((
            (cot_hbm, cot_ref), (fwd_hbm, fwd_ref), (x_hbm, x_ref), (fwdx_hbm, fwdx_ref),
            (permi_hbm, permi_ref), (perm_hbm, perm_ref), (code_hbm, code_ref), (wide_hbm, wide_ref),
            (lat_hbm, lat_ref), (lati_hbm, lati_ref), (narrow_hbm, narrow_ref),
            (latz_hbm, latz_ref), (inv_hbm, inv_ref),
        ))
    ]
    for load in loads:
        load.start()
    loads[0].wait()

    def lanes(p):
        return slice(p * QT, (p + 1) * QT)

    def forward_rows(load):
        def block(r):
            r0 = pl.multiple_of(r * 16, 16)
            u = [load(r0, p) for p in range(PT)]
            s = [None] + [u[p] + u[PT - p] for p in range(1, 6)]
            t = [None] + [u[p] - u[PT - p] for p in range(1, 6)]
            real, imag = real12(u[0], u[6], s, t)
            for i in range(PT):
                k = i if i <= 6 else PT - i
                yr = real[k]
                yi = imag[k]
                c = tw_ref[i : i + 1, :]
                w = tw_ref[PT + i : PT + i + 1, :]
                if yi is None:
                    ar, ai = yr * c, -(yr * w)
                elif i <= 6:
                    ar, ai = yr * c + yi * w, yi * c - yr * w
                else:
                    ar, ai = yr * c - yi * w, -(yi * c) - yr * w
                rows = pl.ds(pl.multiple_of(i * CH + r0, 16), 16)
                ybuf[rows, 0:QT] = ar.astype(BF)
                ybuf[rows, QT : 2 * QT] = ai.astype(BF)

        each(CH // 16, block)

    def dft_chunk(table, c):
        return dot_nt(table[...], ybuf[pl.ds(c * LC, LC), :])

    forward_rows(lambda r0, p: cot_ref[0, pl.ds(r0, 16), lanes(p)].astype(F32))
    loads[1].wait()
    for c in range(CK):
        out = dft_chunk(fwd_ref, c)
        if c == 0:
            row = lax.broadcasted_iota(jnp.int32, out.shape, 0)
            lane = lax.broadcasted_iota(jnp.int32, out.shape, 1)
            first = ((row == 0) | (row == NJ)) & (lane < CH)
            out = out * jnp.where(first, 0.5, 1.0)
        zs[0, c] = out.astype(BF).reshape(NZ, 16, LC)
        if c == 0:
            pl.semaphore_wait(barrier, NZ - 1 + NJ - 1 + 3)
        z_exchange(zs.at[0, c], zr.at[0, c], zs_sem.at[0, c], zr_sem.at[0, c])

    loads[2].wait()
    for p in range(PT):
        v = x_ref[0, :, lanes(p)].astype(F32)
        total = jnp.sum(v, axis=0, keepdims=True)
        off = v - total * (1.0 / CH)
        r, l = p // 3, (p % 3) * QT
        stat_s[r : r + 1, l : l + QT] = total
        stat_s[4 + r : 5 + r, l : l + QT] = jnp.sum(off * off, axis=0, keepdims=True)
    chan_share(stat_s, stat_r, st_ssem, st_rsem)

    diag = (
        lax.broadcasted_iota(jnp.int32, (CH, CH), 0) == lax.broadcasted_iota(jnp.int32, (CH, CH), 1)
    ).astype(F32)
    gcol[...] = jnp.sum(diag * gain_ref[...], axis=1, keepdims=True)
    for m, w in ((m1, iw_ref), (m2, ow_ref)):
        m[...] = jnp.zeros(m.shape, BF)
        m[0:CH, 0:CH] = w[0, 0]
        m[0:CH, 128 : 128 + CH] = w[0, 1]
        m[128 : 128 + CH, 0:CH] = -w[0, 1]
        m[128 : 128 + CH, 128 : 128 + CH] = w[0, 0]
    bias[...] = jnp.zeros(bias.shape, F32)
    bias[0:1, 0:CH] = ib_ref[0, 0:1, :]
    bias[0:1, 128 : 128 + CH] = ib_ref[0, 1:2, :]
    cm[...] = jnp.zeros(cm.shape, jnp.int32)
    loads[6].wait()
    for i in range(PT):
        cm[i, :, 0:CH] = code_ref[i].T
    p1[...] = jnp.zeros(p1.shape, F32)
    p2[...] = jnp.zeros(p2.shape, F32)
    bsum[...] = jnp.zeros(bsum.shape, F32)

    drain(stat_r.at[pl.ds(0, 3)], st_rsem)
    for p in range(PT):
        r, l = p // 3, (p % 3) * QT
        sums = [stat_r[d, r : r + 1, l : l + QT] for d in range(4)]
        spreads = [stat_r[d, 4 + r : 5 + r, l : l + QT] for d in range(4)]
        mean = (sums[0] + sums[1] + sums[2] + sums[3]) * (1.0 / ALL_CH)
        spread = spreads[0] + spreads[1] + spreads[2] + spreads[3]
        for d in range(4):
            gap = sums[d] * (1.0 / CH) - mean
            spread = spread + CH * gap * gap
        mr[0:1, lanes(p)] = mean
        mr[1:2, lanes(p)] = lax.rsqrt(spread * (1.0 / ALL_CH) + 1e-05)

    def xhat(r0, p):
        v = x_ref[0, pl.ds(r0, 16), lanes(p)].astype(F32)
        return (v - mr[0:1, lanes(p)]) * mr[1:2, lanes(p)]

    forward_rows(lambda r0, p: xhat(r0, p) * gcol[pl.ds(r0, 16), :])
    for k in (3, 4, 5):
        loads[k].wait()
    for c in range(CK):
        xs[1, c] = dft_chunk(fwdx_ref, c).astype(BF).reshape(NJ, 32, LC)
        xy_exchange(xs.at[1, c], xr.at[1, c], xs_sem.at[1, c], xr_sem.at[1, c])

    def ready_input(c):
        xy_done(xr.at[1, c], xr_sem.at[1, c])
        got = xr[1, c].reshape(256, LC)
        zs[1, c] = dot_nn(permi_ref[...], got).astype(BF).reshape(NZ, 16, LC)

    def send_input(c):
        z_exchange(zs.at[1, c], zr.at[1, c], zs_sem.at[1, c], zr_sem.at[1, c])

    def second_exchange(c):
        z_done(zr.at[0, c], zr_sem.at[0, c])
        got = zr[0, c].reshape(256, LC)
        xs[0, c] = dot_nn(perm_ref[...], got).astype(BF).reshape(NJ, 32, LC)
        xy_exchange(xs.at[0, c], xr.at[0, c], xs_sem.at[0, c], xr_sem.at[0, c])

    def latitude_modes(table, pencil):
        spread = dot_nn(pencil.reshape(256, LC), wide_ref[...]).astype(BF)
        return dot_nn(table[...], spread)

    def bit(code, place):
        if place >= 2:
            return jnp.bitwise_and(jnp.right_shift(code, place - 1), 2).astype(F32)
        return jnp.bitwise_and(jnp.right_shift(code, place), 1).astype(F32)

    def mode_rows(c, i):
        return slice((c * MC + i) * 128, (c * MC + i + 1) * 128)

    def masked(dst, rows, value, code, place):
        dst[rows, 0:128] = (value[0] * bit(code, place)).astype(BF)
        dst[rows, 128:256] = (value[1] * bit(code, place + 1)).astype(BF)

    def backward_chunk(c):
        xy_done(xr.at[0, c], xr_sem.at[0, c])
        freq = latitude_modes(lat_ref, xr[0, c])
        for i in range(MC):
            col = slice(i * 128, (i + 1) * 128)
            masked(sg_all, mode_rows(c, i), (freq[0:128, col], freq[128:256, col]), cm[c * MC + i], 2)
        chunk = slice(c * LP, (c + 1) * LP)
        back = dot_nt(sg_all[chunk, :], m2[...])
        for i in range(MC):
            row = slice(i * 128, (i + 1) * 128)
            masked(bh_all, mode_rows(c, i), (back[row, 0:128], back[row, 128:256]), cm[c * MC + i], 0)
        grad = dot_nt(bh_all[chunk, :], m1[...]).astype(BF)
        for i in range(MC):
            row = slice(i * 128, (i + 1) * 128)
            gp[0:128, row] = grad[row, 0:128]
            gp[128:256, row] = grad[row, 128:256]
        spec = dot_nn(lati_ref[...], gp[...]).astype(BF)
        bxs[c] = dot_nn(spec, narrow_ref[...]).astype(BF).reshape(NJ, 32, LC)
        xy_exchange(bxs.at[c], bxr.at[c], bxs_sem.at[c], bxr_sem.at[c])

    def second_back(c):
        xy_done(bxr.at[c], bxr_sem.at[c])
        got = bxr[c].reshape(256, LC)
        bzs[c] = dot_nn(permi_ref[...], got).astype(BF).reshape(NZ, 16, LC)

    def send_back(c):
        z_exchange(bzs.at[c], bzr.at[c], bzs_sem.at[c], bzr_sem.at[c])

    def weight_chunk(c):
        z_done(zr.at[1, c], zr_sem.at[1, c])
        freq = latitude_modes(latz_ref, zr[1, c])
        for i in range(MC):
            row = slice(i * 128, (i + 1) * 128)
            fi[row, 0:128] = freq[0:128, row].astype(BF)
            fi[row, 128:256] = freq[128:256, row].astype(BF)
        pre = dot_nn(fi[...], m1[...]) + bias[0:1, :]
        for i in range(MC):
            row = slice(i * 128, (i + 1) * 128)
            masked(hd, row, (pre[row, 0:128], pre[row, 128:256]), cm[c * MC + i], 0)
        chunk = slice(c * LP, (c + 1) * LP)
        sg, bh = sg_all[chunk, :], bh_all[chunk, :]
        p2[...] += dot_tn(hd[...], sg)
        p1[...] += dot_tn(fi[...], bh)
        bsum[0:1, :] += jnp.sum(bh.astype(F32), axis=0, keepdims=True)
        bsum[1:2, :] += jnp.sum(sg.astype(F32), axis=0, keepdims=True)

    for c in range(CK):
        ready_input(c)
    second_exchange(0)
    send_input(0)
    second_exchange(1)
    send_input(1)
    for k in (7, 8, 9, 10):
        loads[k].wait()
    backward_chunk(0)
    second_exchange(2)
    send_input(2)
    backward_chunk(1)
    second_back(0)
    backward_chunk(2)
    second_back(1)
    loads[11].wait()
    weight_chunk(0)
    send_back(0)
    second_back(2)
    weight_chunk(1)
    send_back(1)
    weight_chunk(2)

    for s, src in ((0, p1), (4, p2)):
        real = src[0:CH, 0:128] + src[128 : 128 + CH, 128:256]
        imag = src[0:CH, 128:256] - src[128 : 128 + CH, 0:128]
        rw[s, 0:48] = real[0:48]
        rw[s + 1, 0:48] = real[48:96]
        rw[s + 2, 0:48] = imag[0:48]
        rw[s + 3, 0:48] = imag[48:96]
    for s in range(NJ):
        rw[s, 48:RW] = jnp.zeros((RW - 48, 128), F32)
    rw[0, 48:49] = bsum[0:1, 0:128]
    rw[0, 49:50] = bsum[0:1, 128:256]
    rw[0, 50:51] = bsum[1:2, 0:128]
    rw[0, 51:52] = bsum[1:2, 128:256]
    xy_exchange(rw, rr1, r1_ssem, r1_rsem)
    send_back(2)

    def inverse_chunk(c):
        z_done(bzr.at[c], bzr_sem.at[c])
        got = bzr[c].reshape(256, LC)
        vbuf[pl.ds(c * LC, LC), :] = dot_tn(got, inv_ref[...])

    loads[12].wait()

    def total(ref, count):
        part = ref[0]
        for s in range(1, count):
            part = part + ref[s]
        return part

    xy_done(rr1, r1_rsem)
    rs[...] = total(rr1, NJ).reshape(NEAR, RP, 128)

    def send_near(t):
        to, dev = near_step(t)
        remote(rs.at[to], rr2.at[near], r2_ssem, r2_rsem, dev)

    each(NEAR - 1, send_near)
    rr2[near] = rs[near]
    rest(rr2, NEAR, r2_rsem)
    rt[...] = total(rr2, NEAR)
    share(far_step, NZ // NEAR, block, rt, rr3, r3_ssem, r3_rsem)
    inverse_chunk(0)
    rest(rr3, NZ // NEAR, r3_rsem)
    ru[...] = total(rr3, NZ // NEAR)
    share(near_step, NEAR, near, ru, rr4, r4_ssem, r4_rsem)
    rest(rr4, NEAR, r4_rsem)
    rv[...] = rr4[...].reshape(RW, 128)
    share(xy_step, NJ, j, rv, rr5, r5_ssem, r5_rsem)
    inverse_chunk(1)
    inverse_chunk(2)

    hacc[...] = jnp.zeros(hacc.shape, F32)
    cacc[...] = jnp.zeros(cacc.shape, F32)

    def inverse_rows(r):
        r0 = pl.multiple_of(r * 16, 16)
        re, im = [], []
        for i in range(PT):
            rows = pl.ds(pl.multiple_of(i * CH + r0, 16), 16)
            vr = vbuf[rows, 0:QT]
            vi = vbuf[rows, QT : 2 * QT]
            c = tw_ref[i : i + 1, :]
            w = tw_ref[PT + i : PT + i + 1, :]
            re.append(vr * c - vi * w)
            im.append(None if i in (0, 6) else vr * w + vi * c)
        s = [None] + [re[i] + re[PT - i] for i in range(1, 6)]
        t = [None] + [im[i] - im[PT - i] for i in range(1, 6)]
        real, imag = real12(re[0], re[6], s, t)
        column = gcol[pl.ds(r0, 16), :]
        for p in range(PT):
            k = p if p <= 6 else PT - p
            v = real[k]
            if imag[k] is not None:
                v = v + imag[k] if p <= 6 else v - imag[k]
            v = v * column
            g_ref[pl.ds(r0, 16), lanes(p)] = v
            hacc[:, lanes(p)] += v
            cacc[:, lanes(p)] += v * xhat(r0, p)

    each(CH // 16, inverse_rows)
    for p in range(PT):
        r, l = p // 3, (p % 3) * QT
        tail_s[r : r + 1, l : l + QT] = jnp.sum(hacc[:, lanes(p)], axis=0, keepdims=True)
        tail_s[4 + r : 5 + r, l : l + QT] = jnp.sum(cacc[:, lanes(p)], axis=0, keepdims=True)
    chan_share(tail_s, tail_r, tl_ssem, tl_rsem)

    xy_done(rr5, r5_rsem)
    scale = 1.0 / math.sqrt(LAT * LON / 2)
    for s in range(4):
        for k in range(2):
            wout_ref[s, k * 48 : (k + 1) * 48] = rr5[2 * s + k, 0:48] * scale
    bout_ref[0:4] = rr5[0, 48:52] * scale
    product = jnp.zeros((CH, CH), F32)
    for k in range(2):
        product = product + wout_ref[k, :, 0:CH] * iw_ref[0, k].astype(F32)
    column = jnp.sum(product, axis=1, keepdims=True)
    as_row = jnp.sum(diag * column, axis=0, keepdims=True)
    bout_ref[4:5, 0:CH] = as_row * (1.0 / math.sqrt(LAT * LON) / scale) / gain_ref[...]

    drain(tail_r.at[pl.ds(0, 3)], tl_rsem)
    for p in range(PT):
        r, l = p // 3, (p % 3) * QT
        for k in range(2):
            q = 4 * k + r
            total = tail_r[0, q : q + 1, l : l + QT]
            for d in range(1, 4):
                total = total + tail_r[d, q : q + 1, l : l + QT]
            mr[2 + k : 3 + k, lanes(p)] = total * (1.0 / ALL_CH)
    cell_ref[...] = mr[...]

    for c in range(CK):
        for f in range(2):
            z_done(zs.at[f, c], zs_sem.at[f, c])
            xy_done(xs.at[f, c], xs_sem.at[f, c])
        xy_done(bxs.at[c], bxs_sem.at[c])
        z_done(bzs.at[c], bzs_sem.at[c])
    drain(stat_r.at[pl.ds(0, 3)], st_ssem)
    drain(tail_r.at[pl.ds(0, 3)], tl_ssem)
    xy_done(rw, r1_ssem)
    rest(rr2, NEAR, r2_ssem)
    rest(rr3, NZ // NEAR, r3_ssem)
    rest(rr4, NEAR, r4_ssem)
    xy_done(rr5, r5_ssem)


def finish(
    x_ref, g_ref, cell_ref, w_ref, b_ref, gin_ref, giw_ref, gib_ref, gow_ref, gob_ref, gg_ref
):
    mean, rstd = cell_ref[0:1, :], cell_ref[1:2, :]
    normed = (x_ref[0].astype(F32) - mean) * rstd
    value = g_ref[...] - cell_ref[2:3, :] - normed * cell_ref[3:4, :]
    gin_ref[0] = (value * rstd).astype(BF)

    @pl.when(pl.program_id(0) == 0)
    def _():
        for k in range(2):
            giw_ref[0, k] = w_ref[k, :, 0:CH]
            gow_ref[0, k] = w_ref[2 + k, :, 0:CH]
        gib_ref[0] = b_ref[0:2, 0:CH]
        gob_ref[0] = b_ref[2:4, 0:CH]
        gg_ref[...] = b_ref[4:5, 0:CH]


def per_device(field, cot, gain, inner_w, inner_b, outer_w, codes):
    vm = pl.BlockSpec(memory_space=pltpu.VMEM)
    hbm = pl.BlockSpec(memory_space=pl.ANY)
    *tabs, twiddle = [jnp.asarray(t) for t in tables()]
    codes = codes.transpose(1, 2, 0)
    S = jax.ShapeDtypeStruct
    dma = pltpu.SemaphoreType.DMA
    V = pltpu.VMEM
    loaded = [V(a.shape, a.dtype) for a in (field, cot, codes, *tabs)]
    scratch = loaded + [
        dma((len(loaded),)),
        V((PT * CH, 2 * QT), BF),
        V((2, CK, NZ, 16, LC), BF), V((2, CK, NZ, 16, LC), BF),
        V((2, CK, NJ, 32, LC), BF), V((2, CK, NJ, 32, LC), BF),
        V((CK, NJ, 32, LC), BF), V((CK, NJ, 32, LC), BF),
        V((CK, NZ, 16, LC), BF), V((CK, NZ, 16, LC), BF),
        V((8, 768), F32), V((4, 8, 768), F32), V((8, 768), F32), V((4, 8, 768), F32),
        V((8, LON), F32), V((CH, 1), F32),
        V((256, 256), BF), V((256, 256), BF), V((8, 256), F32), V((PT, 128, 128), jnp.int32),
        V((PT * 128, 256), BF), V((PT * 128, 256), BF), V((LP, 256), BF), V((LP, 256), BF),
        V((256, LP), BF), V((256, 256), F32), V((256, 256), F32), V((8, 256), F32),
        V((PT * CH, 2 * QT), F32), V((16, LON), F32), V((16, LON), F32),
        V((NJ, RW, 128), F32), V((NJ, RW, 128), F32),
        V((NEAR, RP, 128), F32), V((NEAR, RP, 128), F32), V((RP, 128), F32),
        V((NZ // NEAR, RP, 128), F32), V((RP, 128), F32), V((NEAR, RP, 128), F32),
        V((RW, 128), F32), V((NJ, RW, 128), F32),
        dma((2, CK)), dma((2, CK)), dma((2, CK)), dma((2, CK)),
        dma((CK,)), dma((CK,)), dma((CK,)), dma((CK,)),
    ] + [dma(())] * 14
    gain_row = gain.reshape(1, CH)
    grad, cells, weights, small = pl.pallas_call(
        kernel,
        out_shape=(
            S((CH, LON), F32),
            S((8, LON), F32),
            S((4, CH, 128), F32),
            S((8, 128), F32),
        ),
        in_specs=[hbm] * 13 + [vm] * 5,
        out_specs=(vm,) * 4,
        scratch_shapes=scratch,
        compiler_params=pltpu.CompilerParams(
            collective_id=0, has_side_effects=True, vmem_limit_bytes=56 * 2**20
        ),
        name="mixing_backward",
    )(field, cot, codes, *tabs, gain_row, inner_w, inner_b, outer_w, twiddle)
    def fixed(*shape):
        return pl.BlockSpec(shape, lambda i: (0,) * len(shape))

    outs = pl.pallas_call(
        finish,
        out_shape=(
            S((1, CH, LON), BF),
            S((1, 2, CH, CH), F32),
            S((1, 2, CH), F32),
            S((1, 2, CH, CH), F32),
            S((1, 2, CH), F32),
            S((1, CH), F32),
        ),
        grid=(CH // FR,),
        in_specs=[
            pl.BlockSpec((1, FR, LON), lambda i: (0, i, 0)),
            pl.BlockSpec((FR, LON), lambda i: (i, 0)),
            fixed(8, LON),
            fixed(4, CH, 128),
            fixed(8, 128),
        ],
        out_specs=(
            pl.BlockSpec((1, FR, LON), lambda i: (0, i, 0)),
            fixed(1, 2, CH, CH),
            fixed(1, 2, CH),
            fixed(1, 2, CH, CH),
            fixed(1, 2, CH),
            fixed(1, CH),
        ),
        compiler_params=pltpu.CompilerParams(dimension_semantics=("arbitrary",)),
        name="finish",
    )(field, grad, cells, weights, small)
    return outs[:5] + (outs[5].reshape(CH),)


def solution(mesh):
    in_specs = (
        P("lat", "chan", None),
        P("lat", "chan", None),
        P("chan"),
        P("chan", None, None, None),
        P("chan", None, None),
        P("chan", None, None, None),
        P(None, "lat", "chan"),
    )
    out_specs = (
        P("lat", "chan", None),
        P("chan", None, None, None),
        P("chan", None, None),
        P("chan", None, None, None),
        P("chan", None, None),
        P("chan"),
    )
    return jax.shard_map(
        per_device, mesh=mesh, in_specs=in_specs, out_specs=out_specs, check_vma=False
    )
```

```python
import math

import jax
import jax.numpy as jnp
import ml_dtypes
import numpy as np
from jax import lax
from jax.experimental import pallas as pl
from jax.experimental.pallas import tpu as pltpu
from jax.sharding import PartitionSpec as P

MESH = pl.DeviceIdType.MESH
BF = jnp.bfloat16
F32 = jnp.float32

LON = 3072
PT = 12
QT = 256
LAT = 128
CH = 96
ALL_CH = 384
NZ = 16
NJ = 8
CK = 3
MC = PT // CK
LC = MC * CH
LP = MC * 128
RW = 48
FR = 48
NEAR = 4
RP = RW // NEAR


def tables():
    z, p, j = np.meshgrid(np.arange(NZ), np.arange(2), np.arange(NJ), indexing="ij")
    dev = ((j // 4) * 64 + z * 4 + j % 4).reshape(-1)
    part = p.reshape(-1)
    q = np.arange(QT)
    ang = 2 * np.pi * ((dev[:, None] * q[None, :]) % QT) / QT
    cos, sin = np.cos(ang), np.sin(ang)
    re = part[:, None] == 0
    fwd = np.concatenate([np.where(re, cos, -sin), np.where(re, sin, cos)], 1)
    inv = np.concatenate([np.where(re, cos, -sin), np.where(re, sin, cos)], 1)
    j2, p2, z2 = np.meshgrid(np.arange(NJ), np.arange(2), np.arange(NZ), indexing="ij")
    dev2 = ((j2 // 4) * 64 + z2 * 4 + j2 % 4).reshape(-1)
    part2 = p2.reshape(-1)
    mode = np.arange(LAT)
    ang2 = 2 * np.pi * ((mode[:, None] * dev2[None, :]) % LAT) / LAT
    c2, s2 = np.cos(ang2), np.sin(ang2)
    re2 = part2[None, :] == 0
    lat = np.concatenate([np.where(re2, c2, s2), np.where(re2, -s2, c2)], 0) / math.sqrt(LAT)
    pos = (z2 * 2 * NJ + p2 * NJ + j2).reshape(-1)
    perm = np.zeros((256, 256))
    perm[np.arange(256), pos] = 1.0
    widen = np.zeros((LC, LP))
    for i in range(MC):
        widen[i * CH + np.arange(CH), i * 128 + np.arange(CH)] = 1.0
    turn = 2 * np.pi * np.arange(PT)[:, None] * q[None, :] / LON
    twiddle = np.concatenate([np.cos(turn), np.sin(turn)], 0) / math.sqrt(LON)
    order = (fwd, perm @ fwd, inv, lat, lat @ perm, lat.T, perm, perm.T, widen, widen.T)
    bf = [a.astype(ml_dtypes.bfloat16) for a in order]
    return bf + [twiddle.astype(np.float32)]


def real12(u0, u6, s, t):
    h = 0.5
    r3 = math.sqrt(3.0) / 2
    ap, am = u0 + u6, u0 - u6
    s24, d24 = s[2] + s[4], s[2] - s[4]
    s15, d15 = s[1] + s[5], s[1] - s[5]
    e0, o0 = ap + s24, s15 + s[3]
    e1, o1 = am + h * d24, r3 * d15
    e2, o2 = ap - h * s24, h * s15 - s[3]
    real = [e0 + o0, e1 + o1, e2 + o2, am - d24, e2 - o2, e1 - o1, e0 - o0]
    t15, f15 = t[1] + t[5], t[1] - t[5]
    t24, f24 = t[2] + t[4], t[2] - t[4]
    a1, b1 = h * t15 + t[3], r3 * t24
    a2, b2 = r3 * f15, r3 * f24
    imag = [None, -(a1 + b1), -(a2 + b2), t[3] - t15, b2 - a2, b1 - a1, None]
    return real, imag


def dot_nn(a, b):
    return lax.dot_general(a, b, (((1,), (0,)), ((), ())), preferred_element_type=F32)


def dot_nt(a, b):
    return lax.dot_general(a, b, (((1,), (1,)), ((), ())), preferred_element_type=F32)


def dot_tn(a, b):
    return lax.dot_general(a, b, (((0,), (0,)), ((), ())), preferred_element_type=F32)


def kernel(
    x_hbm, cot_hbm, code_hbm, fwd_hbm, fwdx_hbm, inv_hbm, lat_hbm, latz_hbm, lati_hbm,
    perm_hbm, permi_hbm, wide_hbm, narrow_hbm,
    gain_ref, iw_ref, ib_ref, ow_ref, tw_ref,
    g_ref, cell_ref, wout_ref, bout_ref,
    x_ref, cot_ref, code_ref, fwd_ref, fwdx_ref, inv_ref, lat_ref, latz_ref, lati_ref,
    perm_ref, permi_ref, wide_ref, narrow_ref, load_sem,
    ybuf, zs, zr, xs, xr, bxs, bxr, bzs, bzr,
    stat_s, stat_r, tail_s, tail_r, mr, gcol,
    m1, m2, bias, cm, sg_all, bh_all, fi, hd, gp, p1, p2, bsum,
    vbuf, hacc, cacc,
    rw, rr1, rs, rr2, rt, rr3, ru, rr4, rv, rr5,
    zs_sem, zr_sem, xs_sem, xr_sem, bxs_sem, bxr_sem, bzs_sem, bzr_sem,
    st_ssem, st_rsem, tl_ssem, tl_rsem,
    r1_ssem, r1_rsem, r2_ssem, r2_rsem, r3_ssem, r3_rsem, r4_ssem, r4_rsem, r5_ssem, r5_rsem,
):
    me = lax.axis_index("lat")
    chan = lax.axis_index("chan")
    x = me // 64
    z = lax.rem(me // 4, NZ)
    y = lax.rem(me, 4)
    j = x * 4 + y
    base_z = me - z * 4

    def z_step(t):
        half = t // 2
        odd = lax.rem(t, 2)
        off = (half + 1) * (1 - odd) + (NZ - 1 - half) * odd
        to = lax.rem(z + off, NZ)
        return to, {"lat": base_z + to * 4}

    def xy_step(t):
        d = t + 1
        tx = lax.rem(x + d // 4, 2)
        ty = lax.rem(y + lax.rem(d, 4), 4)
        return tx * 4 + ty, {"lat": tx * 64 + z * 4 + ty}

    near, block = lax.rem(z, NEAR), z // NEAR

    def near_step(t):
        to = lax.rem(near + t + 1, NEAR)
        return to, {"lat": base_z + (block * NEAR + to) * 4}

    def far_step(t):
        to = lax.rem(block + t + 1, NZ // NEAR)
        return to, {"lat": base_z + (to * NEAR + near) * 4}

    def chan_step(t):
        to = lax.rem(chan + t + 1, 4)
        return to, {"chan": to}

    def each(count, body):
        def one(t, carry):
            body(t)
            return carry

        lax.fori_loop(0, count, one, 0)

    def remote(src, dst, ssem, rsem, to):
        pltpu.make_async_remote_copy(
            src_ref=src, dst_ref=dst, send_sem=ssem, recv_sem=rsem, device_id=to, device_id_type=MESH
        ).start()

    def drain(ref, sem):
        pltpu.make_async_copy(ref, ref, sem).wait()

    def z_exchange(src, dst, ssem, rsem):
        def send(t):
            to, dev = z_step(t)
            remote(src.at[to], dst.at[z], ssem, rsem, dev)

        each(NZ - 1, send)
        dst[z] = src[z]

    def xy_exchange(src, dst, ssem, rsem):
        def send(t):
            to, dev = xy_step(t)
            remote(src.at[to], dst.at[j], ssem, rsem, dev)

        each(NJ - 1, send)
        dst[j] = src[j]

    def share(step, count, place, src, dst, ssem, rsem):
        def send(t):
            _, dev = step(t)
            remote(src, dst.at[place], ssem, rsem, dev)

        each(count - 1, send)
        dst[place] = src[...]

    def chan_share(src, dst, ssem, rsem):
        share(chan_step, 4, chan, src, dst, ssem, rsem)

    def rest(ref, count, sem):
        drain(ref.at[pl.ds(0, count - 1)], sem)

    def z_done(ref, sem):
        drain(ref.at[pl.ds(0, NZ - 1)], sem)

    def xy_done(ref, sem):
        drain(ref.at[pl.ds(0, NJ - 1)], sem)

    barrier = pltpu.get_barrier_semaphore()

    def greet(step):
        def one(t):
            _, dev = step(t)
            pl.semaphore_signal(barrier, inc=1, device_id=dev, device_id_type=MESH)

        return one

    each(NZ - 1, greet(lambda t: z_step(NZ - 2 - t)))
    each(NJ - 1, greet(xy_step))
    each(3, greet(chan_step))

    loads = [
        pltpu.make_async_copy(src, dst, load_sem.at[k])
        for k, (src, dst) in enumerate((
            (cot_hbm, cot_ref), (fwd_hbm, fwd_ref), (x_hbm, x_ref), (fwdx_hbm, fwdx_ref),
            (permi_hbm, permi_ref), (perm_hbm, perm_ref), (code_hbm, code_ref), (wide_hbm, wide_ref),
            (lat_hbm, lat_ref), (lati_hbm, lati_ref), (narrow_hbm, narrow_ref),
            (latz_hbm, latz_ref), (inv_hbm, inv_ref),
        ))
    ]
    for load in loads:
        load.start()
    loads[0].wait()

    def lanes(p):
        return slice(p * QT, (p + 1) * QT)

    def forward_rows(load):
        def block(r):
            r0 = pl.multiple_of(r * 16, 16)
            u = [load(r0, p) for p in range(PT)]
            s = [None] + [u[p] + u[PT - p] for p in range(1, 6)]
            t = [None] + [u[p] - u[PT - p] for p in range(1, 6)]
            real, imag = real12(u[0], u[6], s, t)
            for i in range(PT):
                k = i if i <= 6 else PT - i
                yr = real[k]
                yi = imag[k]
                c = tw_ref[i : i + 1, :]
                w = tw_ref[PT + i : PT + i + 1, :]
                if yi is None:
                    ar, ai = yr * c, -(yr * w)
                elif i <= 6:
                    ar, ai = yr * c + yi * w, yi * c - yr * w
                else:
                    ar, ai = yr * c - yi * w, -(yi * c) - yr * w
                rows = pl.ds(pl.multiple_of(i * CH + r0, 16), 16)
                ybuf[rows, 0:QT] = ar.astype(BF)
                ybuf[rows, QT : 2 * QT] = ai.astype(BF)

        each(CH // 16, block)

    def dft_chunk(table, c):
        return dot_nt(table[...], ybuf[pl.ds(c * LC, LC), :])

    forward_rows(lambda r0, p: cot_ref[0, pl.ds(r0, 16), lanes(p)].astype(F32))
    loads[1].wait()
    for c in range(CK):
        out = dft_chunk(fwd_ref, c)
        if c == 0:
            row = lax.broadcasted_iota(jnp.int32, out.shape, 0)
            lane = lax.broadcasted_iota(jnp.int32, out.shape, 1)
            first = ((row == 0) | (row == NJ)) & (lane < CH)
            out = out * jnp.where(first, 0.5, 1.0)
        zs[0, c] = out.astype(BF).reshape(NZ, 16, LC)
        if c == 0:
            pl.semaphore_wait(barrier, NZ - 1 + NJ - 1 + 3)
        z_exchange(zs.at[0, c], zr.at[0, c], zs_sem.at[0, c], zr_sem.at[0, c])

    loads[2].wait()
    for p in range(PT):
        v = x_ref[0, :, lanes(p)].astype(F32)
        total = jnp.sum(v, axis=0, keepdims=True)
        off = v - total * (1.0 / CH)
        r, l = p // 3, (p % 3) * QT
        stat_s[r : r + 1, l : l + QT] = total
        stat_s[4 + r : 5 + r, l : l + QT] = jnp.sum(off * off, axis=0, keepdims=True)
    chan_share(stat_s, stat_r, st_ssem, st_rsem)

    diag = (
        lax.broadcasted_iota(jnp.int32, (CH, CH), 0) == lax.broadcasted_iota(jnp.int32, (CH, CH), 1)
    ).astype(F32)
    gcol[...] = jnp.sum(diag * gain_ref[...], axis=1, keepdims=True)
    for m, w in ((m1, iw_ref), (m2, ow_ref)):
        m[...] = jnp.zeros(m.shape, BF)
        m[0:CH, 0:CH] = w[0, 0]
        m[0:CH, 128 : 128 + CH] = w[0, 1]
        m[128 : 128 + CH, 0:CH] = -w[0, 1]
        m[128 : 128 + CH, 128 : 128 + CH] = w[0, 0]
    bias[...] = jnp.zeros(bias.shape, F32)
    bias[0:1, 0:CH] = ib_ref[0, 0:1, :]
    bias[0:1, 128 : 128 + CH] = ib_ref[0, 1:2, :]
    cm[...] = jnp.zeros(cm.shape, jnp.int32)
    loads[6].wait()
    for i in range(PT):
        cm[i, :, 0:CH] = code_ref[i].T
    p1[...] = jnp.zeros(p1.shape, F32)
    p2[...] = jnp.zeros(p2.shape, F32)
    bsum[...] = jnp.zeros(bsum.shape, F32)

    drain(stat_r.at[pl.ds(0, 3)], st_rsem)
    for p in range(PT):
        r, l = p // 3, (p % 3) * QT
        sums = [stat_r[d, r : r + 1, l : l + QT] for d in range(4)]
        spreads = [stat_r[d, 4 + r : 5 + r, l : l + QT] for d in range(4)]
        mean = (sums[0] + sums[1] + sums[2] + sums[3]) * (1.0 / ALL_CH)
        spread = spreads[0] + spreads[1] + spreads[2] + spreads[3]
        for d in range(4):
            gap = sums[d] * (1.0 / CH) - mean
            spread = spread + CH * gap * gap
        mr[0:1, lanes(p)] = mean
        mr[1:2, lanes(p)] = lax.rsqrt(spread * (1.0 / ALL_CH) + 1e-05)

    def xhat(r0, p):
        v = x_ref[0, pl.ds(r0, 16), lanes(p)].astype(F32)
        return (v - mr[0:1, lanes(p)]) * mr[1:2, lanes(p)]

    forward_rows(lambda r0, p: xhat(r0, p) * gcol[pl.ds(r0, 16), :])
    for k in (3, 4, 5):
        loads[k].wait()
    for c in range(CK):
        xs[1, c] = dft_chunk(fwdx_ref, c).astype(BF).reshape(NJ, 32, LC)
        xy_exchange(xs.at[1, c], xr.at[1, c], xs_sem.at[1, c], xr_sem.at[1, c])

    def ready_input(c):
        xy_done(xr.at[1, c], xr_sem.at[1, c])
        got = xr[1, c].reshape(256, LC)
        zs[1, c] = dot_nn(permi_ref[...], got).astype(BF).reshape(NZ, 16, LC)

    def send_input(c):
        z_exchange(zs.at[1, c], zr.at[1, c], zs_sem.at[1, c], zr_sem.at[1, c])

    def second_exchange(c):
        z_done(zr.at[0, c], zr_sem.at[0, c])
        got = zr[0, c].reshape(256, LC)
        xs[0, c] = dot_nn(perm_ref[...], got).astype(BF).reshape(NJ, 32, LC)
        xy_exchange(xs.at[0, c], xr.at[0, c], xs_sem.at[0, c], xr_sem.at[0, c])

    def latitude_modes(table, pencil):
        spread = dot_nn(pencil.reshape(256, LC), wide_ref[...]).astype(BF)
        return dot_nn(table[...], spread)

    def bit(code, place):
        if place >= 2:
            return jnp.bitwise_and(jnp.right_shift(code, place - 1), 2).astype(F32)
        return jnp.bitwise_and(jnp.right_shift(code, place), 1).astype(F32)

    def mode_rows(c, i):
        return slice((c * MC + i) * 128, (c * MC + i + 1) * 128)

    def masked(dst, rows, value, code, place):
        dst[rows, 0:128] = (value[0] * bit(code, place)).astype(BF)
        dst[rows, 128:256] = (value[1] * bit(code, place + 1)).astype(BF)

    def backward_chunk(c):
        xy_done(xr.at[0, c], xr_sem.at[0, c])
        freq = latitude_modes(lat_ref, xr[0, c])
        for i in range(MC):
            col = slice(i * 128, (i + 1) * 128)
            masked(sg_all, mode_rows(c, i), (freq[0:128, col], freq[128:256, col]), cm[c * MC + i], 2)
        chunk = slice(c * LP, (c + 1) * LP)
        back = dot_nt(sg_all[chunk, :], m2[...])
        for i in range(MC):
            row = slice(i * 128, (i + 1) * 128)
            masked(bh_all, mode_rows(c, i), (back[row, 0:128], back[row, 128:256]), cm[c * MC + i], 0)
        grad = dot_nt(bh_all[chunk, :], m1[...]).astype(BF)
        for i in range(MC):
            row = slice(i * 128, (i + 1) * 128)
            gp[0:128, row] = grad[row, 0:128]
            gp[128:256, row] = grad[row, 128:256]
        spec = dot_nn(lati_ref[...], gp[...]).astype(BF)
        bxs[c] = dot_nn(spec, narrow_ref[...]).astype(BF).reshape(NJ, 32, LC)
        xy_exchange(bxs.at[c], bxr.at[c], bxs_sem.at[c], bxr_sem.at[c])
        bsum[0:1, :] += jnp.sum(bh_all[chunk, :].astype(F32), axis=0, keepdims=True)
        bsum[1:2, :] += jnp.sum(sg_all[chunk, :].astype(F32), axis=0, keepdims=True)

    def second_back(c):
        xy_done(bxr.at[c], bxr_sem.at[c])
        got = bxr[c].reshape(256, LC)
        bzs[c] = dot_nn(permi_ref[...], got).astype(BF).reshape(NZ, 16, LC)

    def send_back(c):
        z_exchange(bzs.at[c], bzr.at[c], bzs_sem.at[c], bzr_sem.at[c])

    def weight_chunk(c):
        z_done(zr.at[1, c], zr_sem.at[1, c])
        freq = latitude_modes(latz_ref, zr[1, c])
        for i in range(MC):
            row = slice(i * 128, (i + 1) * 128)
            fi[row, 0:128] = freq[0:128, row].astype(BF)
            fi[row, 128:256] = freq[128:256, row].astype(BF)
        pre = dot_nn(fi[...], m1[...]) + bias[0:1, :]
        for i in range(MC):
            row = slice(i * 128, (i + 1) * 128)
            masked(hd, row, (pre[row, 0:128], pre[row, 128:256]), cm[c * MC + i], 0)
        chunk = slice(c * LP, (c + 1) * LP)
        sg, bh = sg_all[chunk, :], bh_all[chunk, :]
        p2[...] += dot_tn(hd[...], sg)
        p1[...] += dot_tn(fi[...], bh)

    for c in range(CK):
        ready_input(c)
    second_exchange(0)
    send_input(0)
    second_exchange(1)
    send_input(1)
    for k in (7, 8, 9, 10):
        loads[k].wait()
    backward_chunk(0)
    second_exchange(2)
    send_input(2)
    backward_chunk(1)
    second_back(0)
    backward_chunk(2)
    second_back(1)
    loads[11].wait()
    weight_chunk(0)
    second_back(2)
    weight_chunk(1)
    send_back(0)
    weight_chunk(2)

    for s, src in ((0, p1), (4, p2)):
        real = src[0:CH, 0:128] + src[128 : 128 + CH, 128:256]
        imag = src[0:CH, 128:256] - src[128 : 128 + CH, 0:128]
        rw[s, 0:48] = real[0:48]
        rw[s + 1, 0:48] = real[48:96]
        rw[s + 2, 0:48] = imag[0:48]
        rw[s + 3, 0:48] = imag[48:96]
    for r in range(4):
        for k in range(3):
            l = (r % 2) * 128 + 32 * k
            rw[0, 3 * r + k : 3 * r + k + 1, CH:128] = bsum[r // 2 : r // 2 + 1, l : l + 32]
    xy_exchange(rw, rr1, r1_ssem, r1_rsem)
    send_back(1)

    def inverse_chunk(c):
        z_done(bzr.at[c], bzr_sem.at[c])
        got = bzr[c].reshape(256, LC)
        out = dot_tn(got, inv_ref[...])
        for k in range(MC):
            i = c * MC + k
            vr = out[k * CH : (k + 1) * CH, 0:QT]
            vi = out[k * CH : (k + 1) * CH, QT : 2 * QT]
            co = tw_ref[i : i + 1, :]
            si = tw_ref[PT + i : PT + i + 1, :]
            vbuf[i * CH : (i + 1) * CH, 0:QT] = vr * co - vi * si
            if i not in (0, 6):
                vbuf[i * CH : (i + 1) * CH, QT : 2 * QT] = vr * si + vi * co

    loads[12].wait()

    def total(ref, count):
        part = ref[0]
        for s in range(1, count):
            part = part + ref[s]
        return part

    xy_done(rr1, r1_rsem)
    part = total(rr1, NJ)
    rs[...] = jnp.zeros(rs.shape, F32)
    for k in range(NEAR):
        rs[k, 0:RP] = part[k * RP : (k + 1) * RP]

    def send_near(t):
        to, dev = near_step(t)
        remote(rs.at[to], rr2.at[near], r2_ssem, r2_rsem, dev)

    each(NEAR - 1, send_near)
    rr2[near] = rs[near]
    rest(rr2, NEAR, r2_rsem)
    rt[...] = total(rr2, NEAR)
    share(far_step, NZ // NEAR, block, rt, rr3, r3_ssem, r3_rsem)
    send_back(2)
    inverse_chunk(0)
    inverse_chunk(1)
    rest(rr3, NZ // NEAR, r3_rsem)
    ru[...] = total(rr3, NZ // NEAR)
    share(near_step, NEAR, near, ru, rr4, r4_ssem, r4_rsem)
    rest(rr4, NEAR, r4_rsem)
    for k in range(NEAR):
        rv[k * RP : (k + 1) * RP] = rr4[k, 0:RP]
    share(xy_step, NJ, j, rv, rr5, r5_ssem, r5_rsem)
    inverse_chunk(2)

    hacc[...] = jnp.zeros(hacc.shape, F32)
    cacc[...] = jnp.zeros(cacc.shape, F32)

    half_lanes = [[slice(p * QT + h * 128, p * QT + h * 128 + 128) for p in range(PT)] for h in range(2)]

    for h in range(2):
        at = half_lanes[h]

        def inverse_rows(r):
            r0 = pl.multiple_of(r * 32, 32)
            re, im = [], []
            for i in range(PT):
                rows = pl.ds(pl.multiple_of(i * CH + r0, 32), 32)
                re.append(vbuf[rows, h * 128 : h * 128 + 128])
                im.append(None if i in (0, 6) else vbuf[rows, QT + h * 128 : QT + h * 128 + 128])
            s = [None] + [re[i] + re[PT - i] for i in range(1, 6)]
            t = [None] + [im[i] - im[PT - i] for i in range(1, 6)]
            real, imag = real12(re[0], re[6], s, t)
            column = gcol[pl.ds(r0, 32), :]
            for p in range(PT):
                k = p if p <= 6 else PT - p
                v = real[k]
                if imag[k] is not None:
                    v = v + imag[k] if p <= 6 else v - imag[k]
                v = v * column
                g_ref[pl.ds(r0, 32), at[p]] = v
                field = x_ref[0, pl.ds(r0, 32), at[p]].astype(F32)
                w = v * ((field - mr[0:1, at[p]]) * mr[1:2, at[p]])
                hacc[:, at[p]] += (v[0:8] + v[8:16]) + (v[16:24] + v[24:32])
                cacc[:, at[p]] += (w[0:8] + w[8:16]) + (w[16:24] + w[24:32])

        each(CH // 32, inverse_rows)
        for p in range(PT):
            r, l = p // 3, (p % 3) * 128
            tail_s[h, r : r + 1, l : l + 128] = jnp.sum(hacc[:, at[p]], axis=0, keepdims=True)
            tail_s[h, 4 + r : 5 + r, l : l + 128] = jnp.sum(cacc[:, at[p]], axis=0, keepdims=True)
        chan_share(tail_s.at[h], tail_r.at[h], tl_ssem.at[h], tl_rsem.at[h])

    xy_done(rr5, r5_rsem)
    scale = 1.0 / math.sqrt(LAT * LON / 2)
    for s in range(4):
        for k in range(2):
            wout_ref[s, k * 48 : (k + 1) * 48] = rr5[2 * s + k, 0:48] * scale
    for r in range(4):
        for k in range(3):
            row = rr5[0, 3 * r + k : 3 * r + k + 1, CH:128]
            bout_ref[r : r + 1, 32 * k : 32 * k + 32] = row * scale
    product = jnp.zeros((CH, CH), F32)
    for k in range(2):
        product = product + wout_ref[k, :, 0:CH] * iw_ref[0, k].astype(F32)
    column = jnp.sum(product, axis=1, keepdims=True)
    as_row = jnp.sum(diag * column, axis=0, keepdims=True)
    bout_ref[4:5, 0:CH] = as_row * (1.0 / math.sqrt(LAT * LON) / scale) / gain_ref[...]

    for h in range(2):
        drain(tail_r.at[h, pl.ds(0, 3)], tl_rsem.at[h])
        for p in range(PT):
            r, l = p // 3, (p % 3) * 128
            for k in range(2):
                q = 4 * k + r
                whole = tail_r[h, 0, q : q + 1, l : l + 128]
                for d in range(1, 4):
                    whole = whole + tail_r[h, d, q : q + 1, l : l + 128]
                mr[2 + k : 3 + k, half_lanes[h][p]] = whole * (1.0 / ALL_CH)
    cell_ref[...] = mr[...]

    for c in range(CK):
        for f in range(2):
            z_done(zs.at[f, c], zs_sem.at[f, c])
            xy_done(xs.at[f, c], xs_sem.at[f, c])
        xy_done(bxs.at[c], bxs_sem.at[c])
        z_done(bzs.at[c], bzs_sem.at[c])
    drain(stat_r.at[pl.ds(0, 3)], st_ssem)
    for h in range(2):
        drain(tail_r.at[h, pl.ds(0, 3)], tl_ssem.at[h])
    xy_done(rw, r1_ssem)
    rest(rr2, NEAR, r2_ssem)
    rest(rr3, NZ // NEAR, r3_ssem)
    rest(rr4, NEAR, r4_ssem)
    xy_done(rr5, r5_ssem)


def finish(
    x_ref, g_ref, cell_ref, w_ref, b_ref, gin_ref, giw_ref, gib_ref, gow_ref, gob_ref, gg_ref
):
    mean, rstd = cell_ref[0:1, :], cell_ref[1:2, :]
    normed = (x_ref[0].astype(F32) - mean) * rstd
    value = g_ref[...] - cell_ref[2:3, :] - normed * cell_ref[3:4, :]
    gin_ref[0] = (value * rstd).astype(BF)

    @pl.when(pl.program_id(0) == 0)
    def _():
        for k in range(2):
            giw_ref[0, k] = w_ref[k, :, 0:CH]
            gow_ref[0, k] = w_ref[2 + k, :, 0:CH]
        gib_ref[0] = b_ref[0:2, 0:CH]
        gob_ref[0] = b_ref[2:4, 0:CH]
        gg_ref[...] = b_ref[4:5, 0:CH]


def per_device(field, cot, gain, inner_w, inner_b, outer_w, codes):
    vm = pl.BlockSpec(memory_space=pltpu.VMEM)
    hbm = pl.BlockSpec(memory_space=pl.ANY)
    *tabs, twiddle = [jnp.asarray(t) for t in tables()]
    codes = codes.transpose(1, 2, 0)
    S = jax.ShapeDtypeStruct
    dma = pltpu.SemaphoreType.DMA
    V = pltpu.VMEM
    loaded = [V(a.shape, a.dtype) for a in (field, cot, codes, *tabs)]
    scratch = loaded + [
        dma((len(loaded),)),
        V((PT * CH, 2 * QT), BF),
        V((2, CK, NZ, 16, LC), BF), V((2, CK, NZ, 16, LC), BF),
        V((2, CK, NJ, 32, LC), BF), V((2, CK, NJ, 32, LC), BF),
        V((CK, NJ, 32, LC), BF), V((CK, NJ, 32, LC), BF),
        V((CK, NZ, 16, LC), BF), V((CK, NZ, 16, LC), BF),
        V((8, 768), F32), V((4, 8, 768), F32), V((2, 8, 384), F32), V((2, 4, 8, 384), F32),
        V((8, LON), F32), V((CH, 1), F32),
        V((256, 256), BF), V((256, 256), BF), V((8, 256), F32), V((PT, 128, 128), jnp.int32),
        V((PT * 128, 256), BF), V((PT * 128, 256), BF), V((LP, 256), BF), V((LP, 256), BF),
        V((256, LP), BF), V((256, 256), F32), V((256, 256), F32), V((8, 256), F32),
        V((PT * CH, 2 * QT), F32), V((8, LON), F32), V((8, LON), F32),
        V((NJ, RW, 128), F32), V((NJ, RW, 128), F32),
        V((NEAR, 16, 128), F32), V((NEAR, 16, 128), F32), V((16, 128), F32),
        V((NZ // NEAR, 16, 128), F32), V((16, 128), F32), V((NEAR, 16, 128), F32),
        V((RW, 128), F32), V((NJ, RW, 128), F32),
        dma((2, CK)), dma((2, CK)), dma((2, CK)), dma((2, CK)),
        dma((CK,)), dma((CK,)), dma((CK,)), dma((CK,)),
    ] + [dma(()), dma(()), dma((2,)), dma((2,))] + [dma(())] * 10
    gain_row = gain.reshape(1, CH)
    grad, cells, weights, small = pl.pallas_call(
        kernel,
        out_shape=(
            S((CH, LON), F32),
            S((8, LON), F32),
            S((4, CH, 128), F32),
            S((8, 128), F32),
        ),
        in_specs=[hbm] * 13 + [vm] * 5,
        out_specs=(vm,) * 4,
        scratch_shapes=scratch,
        compiler_params=pltpu.CompilerParams(
            collective_id=0, has_side_effects=True, vmem_limit_bytes=56 * 2**20
        ),
        name="mixing_backward",
    )(field, cot, codes, *tabs, gain_row, inner_w, inner_b, outer_w, twiddle)
    def fixed(*shape):
        return pl.BlockSpec(shape, lambda i: (0,) * len(shape))

    outs = pl.pallas_call(
        finish,
        out_shape=(
            S((1, CH, LON), BF),
            S((1, 2, CH, CH), F32),
            S((1, 2, CH), F32),
            S((1, 2, CH, CH), F32),
            S((1, 2, CH), F32),
            S((1, CH), F32),
        ),
        grid=(CH // FR,),
        in_specs=[
            pl.BlockSpec((1, FR, LON), lambda i: (0, i, 0)),
            pl.BlockSpec((FR, LON), lambda i: (i, 0)),
            fixed(8, LON),
            fixed(4, CH, 128),
            fixed(8, 128),
        ],
        out_specs=(
            pl.BlockSpec((1, FR, LON), lambda i: (0, i, 0)),
            fixed(1, 2, CH, CH),
            fixed(1, 2, CH),
            fixed(1, 2, CH, CH),
            fixed(1, 2, CH),
            fixed(1, CH),
        ),
        compiler_params=pltpu.CompilerParams(dimension_semantics=("arbitrary",)),
        name="finish",
    )(field, grad, cells, weights, small)
    return outs[:5] + (outs[5].reshape(CH),)


def solution(mesh):
    in_specs = (
        P("lat", "chan", None),
        P("lat", "chan", None),
        P("chan"),
        P("chan", None, None, None),
        P("chan", None, None),
        P("chan", None, None, None),
        P(None, "lat", "chan"),
    )
    out_specs = (
        P("lat", "chan", None),
        P("chan", None, None, None),
        P("chan", None, None),
        P("chan", None, None, None),
        P("chan", None, None),
        P("chan"),
    )
    return jax.shard_map(
        per_device, mesh=mesh, in_specs=in_specs, out_specs=out_specs, check_vma=False
    )
```

```python
import math

import jax
import jax.numpy as jnp
import ml_dtypes
import numpy as np
from jax import lax
from jax.experimental import pallas as pl
from jax.experimental.pallas import tpu as pltpu
from jax.sharding import PartitionSpec as P

MESH = pl.DeviceIdType.MESH
BF = jnp.bfloat16
F32 = jnp.float32

LON = 3072
PT = 12
QT = 256
LAT = 128
CH = 96
ALL_CH = 384
NZ = 16
NJ = 8
CK = 3
MC = PT // CK
LC = MC * CH
LP = MC * 128
RW = 48
FR = 48
NEAR = 4
RP = RW // NEAR


def tables():
    z, p, j = np.meshgrid(np.arange(NZ), np.arange(2), np.arange(NJ), indexing="ij")
    dev = ((j // 4) * 64 + z * 4 + j % 4).reshape(-1)
    part = p.reshape(-1)
    q = np.arange(QT)
    ang = 2 * np.pi * ((dev[:, None] * q[None, :]) % QT) / QT
    cos, sin = np.cos(ang), np.sin(ang)
    re = part[:, None] == 0
    fwd = np.concatenate([np.where(re, cos, -sin), np.where(re, sin, cos)], 1)
    inv = np.concatenate([np.where(re, cos, -sin), np.where(re, sin, cos)], 1)
    j2, p2, z2 = np.meshgrid(np.arange(NJ), np.arange(2), np.arange(NZ), indexing="ij")
    dev2 = ((j2 // 4) * 64 + z2 * 4 + j2 % 4).reshape(-1)
    part2 = p2.reshape(-1)
    mode = np.arange(LAT)
    ang2 = 2 * np.pi * ((mode[:, None] * dev2[None, :]) % LAT) / LAT
    c2, s2 = np.cos(ang2), np.sin(ang2)
    re2 = part2[None, :] == 0
    lat = np.concatenate([np.where(re2, c2, s2), np.where(re2, -s2, c2)], 0) / math.sqrt(LAT)
    pos = (z2 * 2 * NJ + p2 * NJ + j2).reshape(-1)
    perm = np.zeros((256, 256))
    perm[np.arange(256), pos] = 1.0
    widen = np.zeros((LC, LP))
    for i in range(MC):
        widen[i * CH + np.arange(CH), i * 128 + np.arange(CH)] = 1.0
    turn = 2 * np.pi * np.arange(PT)[:, None] * q[None, :] / LON
    twiddle = np.concatenate([np.cos(turn), np.sin(turn)], 0) / math.sqrt(LON)
    order = (fwd, perm @ fwd, inv, lat, lat @ perm, lat.T, perm, perm.T, widen, widen.T)
    bf = [a.astype(ml_dtypes.bfloat16) for a in order]
    return bf + [twiddle.astype(np.float32)]


def real12(u0, u6, s, t):
    h = 0.5
    r3 = math.sqrt(3.0) / 2
    ap, am = u0 + u6, u0 - u6
    s24, d24 = s[2] + s[4], s[2] - s[4]
    s15, d15 = s[1] + s[5], s[1] - s[5]
    e0, o0 = ap + s24, s15 + s[3]
    e1, o1 = am + h * d24, r3 * d15
    e2, o2 = ap - h * s24, h * s15 - s[3]
    real = [e0 + o0, e1 + o1, e2 + o2, am - d24, e2 - o2, e1 - o1, e0 - o0]
    t15, f15 = t[1] + t[5], t[1] - t[5]
    t24, f24 = t[2] + t[4], t[2] - t[4]
    a1, b1 = h * t15 + t[3], r3 * t24
    a2, b2 = r3 * f15, r3 * f24
    imag = [None, -(a1 + b1), -(a2 + b2), t[3] - t15, b2 - a2, b1 - a1, None]
    return real, imag


def dot_nn(a, b):
    return lax.dot_general(a, b, (((1,), (0,)), ((), ())), preferred_element_type=F32)


def dot_nt(a, b):
    return lax.dot_general(a, b, (((1,), (1,)), ((), ())), preferred_element_type=F32)


def dot_tn(a, b):
    return lax.dot_general(a, b, (((0,), (0,)), ((), ())), preferred_element_type=F32)


def kernel(
    x_hbm, cot_hbm, code_hbm, fwd_hbm, fwdx_hbm, inv_hbm, lat_hbm, latz_hbm, lati_hbm,
    perm_hbm, permi_hbm, wide_hbm, narrow_hbm,
    gain_hbm, iw_hbm, ib_hbm, ow_hbm, tw_hbm,
    g_hbm, cell_ref, wout_ref, bout_ref,
    x_ref, cot_ref, code_ref, fwd_ref, fwdx_ref, inv_ref, lat_ref, latz_ref, lati_ref,
    perm_ref, permi_ref, wide_ref, narrow_ref, gain_ref, iw_ref, ib_ref, ow_ref, tw_ref,
    load_sem, g_ref, g_sem,
    ybuf, zs, zr, xs, xr, bxs, bxr, bzs, bzr,
    stat_s, stat_r, tail_s, tail_r, mr, gcol,
    m1, m2, bias, cm, sg_all, bh_all, fi, hd, gp, p1, p2, bsum,
    vbuf, hacc, cacc,
    rw, rr1, rs, rr2, rt, rr3, ru, rr4, rv, rr5,
    zs_sem, zr_sem, xs_sem, xr_sem, bxs_sem, bxr_sem, bzs_sem, bzr_sem,
    st_ssem, st_rsem, tl_ssem, tl_rsem,
    r1_ssem, r1_rsem, r2_ssem, r2_rsem, r3_ssem, r3_rsem, r4_ssem, r4_rsem, r5_ssem, r5_rsem,
):
    me = lax.axis_index("lat")
    chan = lax.axis_index("chan")
    x = me // 64
    z = lax.rem(me // 4, NZ)
    y = lax.rem(me, 4)
    j = x * 4 + y
    base_z = me - z * 4

    def z_step(t):
        half = t // 2
        odd = lax.rem(t, 2)
        off = (half + 1) * (1 - odd) + (NZ - 1 - half) * odd
        to = lax.rem(z + off, NZ)
        return to, {"lat": base_z + to * 4}

    def xy_step(t):
        d = t + 1
        tx = lax.rem(x + d // 4, 2)
        ty = lax.rem(y + lax.rem(d, 4), 4)
        return tx * 4 + ty, {"lat": tx * 64 + z * 4 + ty}

    near, block = lax.rem(z, NEAR), z // NEAR

    def near_step(t):
        to = lax.rem(near + t + 1, NEAR)
        return to, {"lat": base_z + (block * NEAR + to) * 4}

    def far_step(t):
        to = lax.rem(block + t + 1, NZ // NEAR)
        return to, {"lat": base_z + (to * NEAR + near) * 4}

    def chan_step(t):
        to = lax.rem(chan + t + 1, 4)
        return to, {"chan": to}

    def each(count, body):
        def one(t, carry):
            body(t)
            return carry

        lax.fori_loop(0, count, one, 0)

    def remote(src, dst, ssem, rsem, to):
        pltpu.make_async_remote_copy(
            src_ref=src, dst_ref=dst, send_sem=ssem, recv_sem=rsem, device_id=to, device_id_type=MESH
        ).start()

    def drain(ref, sem):
        pltpu.make_async_copy(ref, ref, sem).wait()

    def z_exchange(src, dst, ssem, rsem):
        def send(t):
            to, dev = z_step(t)
            remote(src.at[to], dst.at[z], ssem, rsem, dev)

        each(NZ - 1, send)
        dst[z] = src[z]

    def xy_exchange(src, dst, ssem, rsem):
        def send(t):
            to, dev = xy_step(t)
            remote(src.at[to], dst.at[j], ssem, rsem, dev)

        each(NJ - 1, send)
        dst[j] = src[j]

    def share(step, count, place, src, dst, ssem, rsem):
        def send(t):
            _, dev = step(t)
            remote(src, dst.at[place], ssem, rsem, dev)

        each(count - 1, send)
        dst[place] = src[...]

    def chan_share(src, dst, ssem, rsem):
        share(chan_step, 4, chan, src, dst, ssem, rsem)

    def rest(ref, count, sem):
        drain(ref.at[pl.ds(0, count - 1)], sem)

    def z_done(ref, sem):
        drain(ref.at[pl.ds(0, NZ - 1)], sem)

    def xy_done(ref, sem):
        drain(ref.at[pl.ds(0, NJ - 1)], sem)

    barrier = pltpu.get_barrier_semaphore()

    def greet(step):
        def one(t):
            _, dev = step(t)
            pl.semaphore_signal(barrier, inc=1, device_id=dev, device_id_type=MESH)

        return one

    each(NZ - 1, greet(lambda t: z_step(NZ - 2 - t)))
    each(NJ - 1, greet(xy_step))
    each(3, greet(chan_step))

    loads = [
        pltpu.make_async_copy(src, dst, load_sem.at[k])
        for k, (src, dst) in enumerate((
            (cot_hbm, cot_ref), (fwd_hbm, fwd_ref), (x_hbm, x_ref), (fwdx_hbm, fwdx_ref),
            (permi_hbm, permi_ref), (perm_hbm, perm_ref), (code_hbm, code_ref), (wide_hbm, wide_ref),
            (lat_hbm, lat_ref), (lati_hbm, lati_ref), (narrow_hbm, narrow_ref),
            (latz_hbm, latz_ref), (inv_hbm, inv_ref), (gain_hbm, gain_ref), (iw_hbm, iw_ref),
            (ib_hbm, ib_ref), (ow_hbm, ow_ref), (tw_hbm, tw_ref),
        ))
    ]
    for load in (loads[17], *loads[:17]):
        load.start()
    loads[17].wait()
    loads[0].wait()

    def lanes(p):
        return slice(p * QT, (p + 1) * QT)

    def forward_rows(load):
        def block(r):
            r0 = pl.multiple_of(r * 16, 16)
            u = [load(r0, p) for p in range(PT)]
            s = [None] + [u[p] + u[PT - p] for p in range(1, 6)]
            t = [None] + [u[p] - u[PT - p] for p in range(1, 6)]
            real, imag = real12(u[0], u[6], s, t)
            for i in range(PT):
                k = i if i <= 6 else PT - i
                yr = real[k]
                yi = imag[k]
                c = tw_ref[i : i + 1, :]
                w = tw_ref[PT + i : PT + i + 1, :]
                if yi is None:
                    ar, ai = yr * c, -(yr * w)
                elif i <= 6:
                    ar, ai = yr * c + yi * w, yi * c - yr * w
                else:
                    ar, ai = yr * c - yi * w, -(yi * c) - yr * w
                rows = pl.ds(pl.multiple_of(i * CH + r0, 16), 16)
                ybuf[rows, 0:QT] = ar.astype(BF)
                ybuf[rows, QT : 2 * QT] = ai.astype(BF)

        each(CH // 16, block)

    def dft_chunk(table, c):
        return dot_nt(table[...], ybuf[pl.ds(c * LC, LC), :])

    forward_rows(lambda r0, p: cot_ref[0, pl.ds(r0, 16), lanes(p)].astype(F32))
    loads[1].wait()
    for c in range(CK):
        out = dft_chunk(fwd_ref, c)
        if c == 0:
            row = lax.broadcasted_iota(jnp.int32, out.shape, 0)
            lane = lax.broadcasted_iota(jnp.int32, out.shape, 1)
            first = ((row == 0) | (row == NJ)) & (lane < CH)
            out = out * jnp.where(first, 0.5, 1.0)
        zs[0, c] = out.astype(BF).reshape(NZ, 16, LC)
        if c == 0:
            pl.semaphore_wait(barrier, NZ - 1 + NJ - 1 + 3)
        z_exchange(zs.at[0, c], zr.at[0, c], zs_sem.at[0, c], zr_sem.at[0, c])

    loads[2].wait()
    for p in range(PT):
        v = x_ref[0, :, lanes(p)].astype(F32)
        total = jnp.sum(v, axis=0, keepdims=True)
        off = v - total * (1.0 / CH)
        r, l = p // 3, (p % 3) * QT
        stat_s[r : r + 1, l : l + QT] = total
        stat_s[4 + r : 5 + r, l : l + QT] = jnp.sum(off * off, axis=0, keepdims=True)
    chan_share(stat_s, stat_r, st_ssem, st_rsem)

    for k in (13, 14, 15, 16):
        loads[k].wait()
    diag = (
        lax.broadcasted_iota(jnp.int32, (CH, CH), 0) == lax.broadcasted_iota(jnp.int32, (CH, CH), 1)
    ).astype(F32)
    gcol[...] = jnp.sum(diag * gain_ref[...], axis=1, keepdims=True)
    for m, w in ((m1, iw_ref), (m2, ow_ref)):
        m[...] = jnp.zeros(m.shape, BF)
        m[0:CH, 0:CH] = w[0, 0]
        m[0:CH, 128 : 128 + CH] = w[0, 1]
        m[128 : 128 + CH, 0:CH] = -w[0, 1]
        m[128 : 128 + CH, 128 : 128 + CH] = w[0, 0]
    bias[...] = jnp.zeros(bias.shape, F32)
    bias[0:1, 0:CH] = ib_ref[0, 0:1, :]
    bias[0:1, 128 : 128 + CH] = ib_ref[0, 1:2, :]
    cm[...] = jnp.zeros(cm.shape, jnp.int32)
    loads[6].wait()
    for i in range(PT):
        cm[i, :, 0:CH] = code_ref[i].T
    p1[...] = jnp.zeros(p1.shape, F32)
    p2[...] = jnp.zeros(p2.shape, F32)
    bsum[...] = jnp.zeros(bsum.shape, F32)

    drain(stat_r.at[pl.ds(0, 3)], st_rsem)
    for p in range(PT):
        r, l = p // 3, (p % 3) * QT
        sums = [stat_r[d, r : r + 1, l : l + QT] for d in range(4)]
        spreads = [stat_r[d, 4 + r : 5 + r, l : l + QT] for d in range(4)]
        mean = (sums[0] + sums[1] + sums[2] + sums[3]) * (1.0 / ALL_CH)
        spread = spreads[0] + spreads[1] + spreads[2] + spreads[3]
        for d in range(4):
            gap = sums[d] * (1.0 / CH) - mean
            spread = spread + CH * gap * gap
        mr[0:1, lanes(p)] = mean
        mr[1:2, lanes(p)] = lax.rsqrt(spread * (1.0 / ALL_CH) + 1e-05)

    def xhat(r0, p):
        v = x_ref[0, pl.ds(r0, 16), lanes(p)].astype(F32)
        return (v - mr[0:1, lanes(p)]) * mr[1:2, lanes(p)]

    forward_rows(lambda r0, p: xhat(r0, p) * gcol[pl.ds(r0, 16), :])
    for k in (3, 4, 5):
        loads[k].wait()
    for c in range(CK):
        xs[1, c] = dft_chunk(fwdx_ref, c).astype(BF).reshape(NJ, 32, LC)
        xy_exchange(xs.at[1, c], xr.at[1, c], xs_sem.at[1, c], xr_sem.at[1, c])

    def ready_input(c):
        xy_done(xr.at[1, c], xr_sem.at[1, c])
        got = xr[1, c].reshape(256, LC)
        zs[1, c] = dot_nn(permi_ref[...], got).astype(BF).reshape(NZ, 16, LC)

    def send_input(c):
        z_exchange(zs.at[1, c], zr.at[1, c], zs_sem.at[1, c], zr_sem.at[1, c])

    def second_exchange(c):
        z_done(zr.at[0, c], zr_sem.at[0, c])
        got = zr[0, c].reshape(256, LC)
        xs[0, c] = dot_nn(perm_ref[...], got).astype(BF).reshape(NJ, 32, LC)
        xy_exchange(xs.at[0, c], xr.at[0, c], xs_sem.at[0, c], xr_sem.at[0, c])

    def latitude_modes(table, pencil):
        spread = dot_nn(pencil.reshape(256, LC), wide_ref[...]).astype(BF)
        return dot_nn(table[...], spread)

    def bit(code, place):
        if place >= 2:
            return jnp.bitwise_and(jnp.right_shift(code, place - 1), 2).astype(F32)
        return jnp.bitwise_and(jnp.right_shift(code, place), 1).astype(F32)

    def mode_rows(c, i):
        return slice((c * MC + i) * 128, (c * MC + i + 1) * 128)

    def masked(dst, rows, value, code, place):
        dst[rows, 0:128] = (value[0] * bit(code, place)).astype(BF)
        dst[rows, 128:256] = (value[1] * bit(code, place + 1)).astype(BF)

    def backward_chunk(c):
        xy_done(xr.at[0, c], xr_sem.at[0, c])
        freq = latitude_modes(lat_ref, xr[0, c])
        for i in range(MC):
            col = slice(i * 128, (i + 1) * 128)
            masked(sg_all, mode_rows(c, i), (freq[0:128, col], freq[128:256, col]), cm[c * MC + i], 2)
        chunk = slice(c * LP, (c + 1) * LP)
        back = dot_nt(sg_all[chunk, :], m2[...])
        for i in range(MC):
            row = slice(i * 128, (i + 1) * 128)
            masked(bh_all, mode_rows(c, i), (back[row, 0:128], back[row, 128:256]), cm[c * MC + i], 0)
        grad = dot_nt(bh_all[chunk, :], m1[...]).astype(BF)
        for i in range(MC):
            row = slice(i * 128, (i + 1) * 128)
            gp[0:128, row] = grad[row, 0:128]
            gp[128:256, row] = grad[row, 128:256]
        spec = dot_nn(lati_ref[...], gp[...]).astype(BF)
        bxs[c] = dot_nn(spec, narrow_ref[...]).astype(BF).reshape(NJ, 32, LC)
        xy_exchange(bxs.at[c], bxr.at[c], bxs_sem.at[c], bxr_sem.at[c])
        bsum[0:1, :] += jnp.sum(bh_all[chunk, :].astype(F32), axis=0, keepdims=True)
        bsum[1:2, :] += jnp.sum(sg_all[chunk, :].astype(F32), axis=0, keepdims=True)

    def second_back(c):
        xy_done(bxr.at[c], bxr_sem.at[c])
        got = bxr[c].reshape(256, LC)
        bzs[c] = dot_nn(permi_ref[...], got).astype(BF).reshape(NZ, 16, LC)

    def send_back(c):
        z_exchange(bzs.at[c], bzr.at[c], bzs_sem.at[c], bzr_sem.at[c])

    def weight_chunk(c):
        z_done(zr.at[1, c], zr_sem.at[1, c])
        if c == CK - 1:
            send_back(1)
        freq = latitude_modes(latz_ref, zr[1, c])
        for i in range(MC):
            row = slice(i * 128, (i + 1) * 128)
            fi[row, 0:128] = freq[0:128, row].astype(BF)
            fi[row, 128:256] = freq[128:256, row].astype(BF)
        pre = dot_nn(fi[...], m1[...]) + bias[0:1, :]
        for i in range(MC):
            row = slice(i * 128, (i + 1) * 128)
            masked(hd, row, (pre[row, 0:128], pre[row, 128:256]), cm[c * MC + i], 0)
        chunk = slice(c * LP, (c + 1) * LP)
        sg, bh = sg_all[chunk, :], bh_all[chunk, :]
        p2[...] += dot_tn(hd[...], sg)
        p1[...] += dot_tn(fi[...], bh)

    for c in range(CK):
        ready_input(c)
    second_exchange(0)
    send_input(0)
    second_exchange(1)
    send_input(1)
    for k in (7, 8, 9, 10):
        loads[k].wait()
    backward_chunk(0)
    second_exchange(2)
    send_input(2)
    backward_chunk(1)
    second_back(0)
    backward_chunk(2)
    second_back(1)
    loads[11].wait()
    weight_chunk(0)
    send_back(0)
    second_back(2)
    weight_chunk(1)
    weight_chunk(2)

    for s, src in ((0, p1), (4, p2)):
        real = src[0:CH, 0:128] + src[128 : 128 + CH, 128:256]
        imag = src[0:CH, 128:256] - src[128 : 128 + CH, 0:128]
        rw[s, 0:48] = real[0:48]
        rw[s + 1, 0:48] = real[48:96]
        rw[s + 2, 0:48] = imag[0:48]
        rw[s + 3, 0:48] = imag[48:96]
    for r in range(4):
        for k in range(3):
            l = (r % 2) * 128 + 32 * k
            rw[0, 3 * r + k : 3 * r + k + 1, CH:128] = bsum[r // 2 : r // 2 + 1, l : l + 32]
    xy_exchange(rw, rr1, r1_ssem, r1_rsem)

    def inverse_chunk(c):
        z_done(bzr.at[c], bzr_sem.at[c])
        got = bzr[c].reshape(256, LC)
        out = dot_tn(got, inv_ref[...])
        for k in range(MC):
            i = c * MC + k
            vr = out[k * CH : (k + 1) * CH, 0:QT]
            vi = out[k * CH : (k + 1) * CH, QT : 2 * QT]
            co = tw_ref[i : i + 1, :]
            si = tw_ref[PT + i : PT + i + 1, :]
            vbuf[i * CH : (i + 1) * CH, 0:QT] = vr * co - vi * si
            if i not in (0, 6):
                vbuf[i * CH : (i + 1) * CH, QT : 2 * QT] = vr * si + vi * co

    loads[12].wait()

    def total(ref, count):
        part = ref[0]
        for s in range(1, count):
            part = part + ref[s]
        return part

    xy_done(rr1, r1_rsem)
    part = total(rr1, NJ)
    rs[...] = jnp.zeros(rs.shape, F32)
    for k in range(NEAR):
        rs[k, 0:RP] = part[k * RP : (k + 1) * RP]

    def send_near(t):
        to, dev = near_step(t)
        remote(rs.at[to], rr2.at[near], r2_ssem, r2_rsem, dev)

    each(NEAR - 1, send_near)
    rr2[near] = rs[near]
    rest(rr2, NEAR, r2_rsem)
    rt[...] = total(rr2, NEAR)
    share(far_step, NZ // NEAR, block, rt, rr3, r3_ssem, r3_rsem)
    send_back(2)
    inverse_chunk(0)
    inverse_chunk(1)
    rest(rr3, NZ // NEAR, r3_rsem)
    ru[...] = total(rr3, NZ // NEAR)
    share(near_step, NEAR, near, ru, rr4, r4_ssem, r4_rsem)
    rest(rr4, NEAR, r4_rsem)
    for k in range(NEAR):
        rv[k * RP : (k + 1) * RP] = rr4[k, 0:RP]
    share(xy_step, NJ, j, rv, rr5, r5_ssem, r5_rsem)
    inverse_chunk(2)

    hacc[...] = jnp.zeros(hacc.shape, F32)
    cacc[...] = jnp.zeros(cacc.shape, F32)

    half_lanes = [[slice(p * QT + h * 128, p * QT + h * 128 + 128) for p in range(PT)] for h in range(2)]

    for h in range(2):
        at = half_lanes[h]

        def inverse_rows(r):
            r0 = pl.multiple_of(r * 32, 32)
            re, im = [], []
            for i in range(PT):
                rows = pl.ds(pl.multiple_of(i * CH + r0, 32), 32)
                re.append(vbuf[rows, h * 128 : h * 128 + 128])
                im.append(None if i in (0, 6) else vbuf[rows, QT + h * 128 : QT + h * 128 + 128])
            s = [None] + [re[i] + re[PT - i] for i in range(1, 6)]
            t = [None] + [im[i] - im[PT - i] for i in range(1, 6)]
            real, imag = real12(re[0], re[6], s, t)
            column = gcol[pl.ds(r0, 32), :]
            for p in range(PT):
                k = p if p <= 6 else PT - p
                v = real[k]
                if imag[k] is not None:
                    v = v + imag[k] if p <= 6 else v - imag[k]
                v = v * column
                g_ref[pl.ds(r0, 32), at[p]] = v
                field = x_ref[0, pl.ds(r0, 32), at[p]].astype(F32)
                w = v * ((field - mr[0:1, at[p]]) * mr[1:2, at[p]])
                hacc[:, at[p]] += (v[0:8] + v[8:16]) + (v[16:24] + v[24:32])
                cacc[:, at[p]] += (w[0:8] + w[8:16]) + (w[16:24] + w[24:32])

        each(CH // 32, inverse_rows)
        for p in range(PT):
            r, l = p // 3, (p % 3) * 128
            tail_s[h, r : r + 1, l : l + 128] = jnp.sum(hacc[:, at[p]], axis=0, keepdims=True)
            tail_s[h, 4 + r : 5 + r, l : l + 128] = jnp.sum(cacc[:, at[p]], axis=0, keepdims=True)
        chan_share(tail_s.at[h], tail_r.at[h], tl_ssem.at[h], tl_rsem.at[h])

    g_copy = pltpu.make_async_copy(g_ref, g_hbm, g_sem)
    g_copy.start()

    xy_done(rr5, r5_rsem)
    scale = 1.0 / math.sqrt(LAT * LON / 2)
    for s in range(4):
        for k in range(2):
            wout_ref[s, k * 48 : (k + 1) * 48] = rr5[2 * s + k, 0:48] * scale
    for r in range(4):
        for k in range(3):
            row = rr5[0, 3 * r + k : 3 * r + k + 1, CH:128]
            bout_ref[r : r + 1, 32 * k : 32 * k + 32] = row * scale
    product = jnp.zeros((CH, CH), F32)
    for k in range(2):
        product = product + wout_ref[k, :, 0:CH] * iw_ref[0, k].astype(F32)
    column = jnp.sum(product, axis=1, keepdims=True)
    as_row = jnp.sum(diag * column, axis=0, keepdims=True)
    bout_ref[4:5, 0:CH] = as_row * (1.0 / math.sqrt(LAT * LON) / scale) / gain_ref[...]

    for h in range(2):
        drain(tail_r.at[h, pl.ds(0, 3)], tl_rsem.at[h])
        for p in range(PT):
            r, l = p // 3, (p % 3) * 128
            for k in range(2):
                q = 4 * k + r
                whole = tail_r[h, 0, q : q + 1, l : l + 128]
                for d in range(1, 4):
                    whole = whole + tail_r[h, d, q : q + 1, l : l + 128]
                mr[2 + k : 3 + k, half_lanes[h][p]] = whole * (1.0 / ALL_CH)
    cell_ref[...] = mr[...]

    g_copy.wait()
    for c in range(CK):
        for f in range(2):
            z_done(zs.at[f, c], zs_sem.at[f, c])
            xy_done(xs.at[f, c], xs_sem.at[f, c])
        xy_done(bxs.at[c], bxs_sem.at[c])
        z_done(bzs.at[c], bzs_sem.at[c])
    drain(stat_r.at[pl.ds(0, 3)], st_ssem)
    for h in range(2):
        drain(tail_r.at[h, pl.ds(0, 3)], tl_ssem.at[h])
    xy_done(rw, r1_ssem)
    rest(rr2, NEAR, r2_ssem)
    rest(rr3, NZ // NEAR, r3_ssem)
    rest(rr4, NEAR, r4_ssem)
    xy_done(rr5, r5_ssem)


def finish(
    x_ref, g_ref, cell_ref, w_ref, b_ref, gin_ref, giw_ref, gib_ref, gow_ref, gob_ref, gg_ref
):
    mean, rstd = cell_ref[0:1, :], cell_ref[1:2, :]
    normed = (x_ref[0].astype(F32) - mean) * rstd
    value = g_ref[...] - cell_ref[2:3, :] - normed * cell_ref[3:4, :]
    gin_ref[0] = (value * rstd).astype(BF)

    @pl.when(pl.program_id(0) == 0)
    def _():
        for k in range(2):
            giw_ref[0, k] = w_ref[k, :, 0:CH]
            gow_ref[0, k] = w_ref[2 + k, :, 0:CH]
        gib_ref[0] = b_ref[0:2, 0:CH]
        gob_ref[0] = b_ref[2:4, 0:CH]
        gg_ref[...] = b_ref[4:5, 0:CH]


def per_device(field, cot, gain, inner_w, inner_b, outer_w, codes):
    vm = pl.BlockSpec(memory_space=pltpu.VMEM)
    hbm = pl.BlockSpec(memory_space=pl.ANY)
    *tabs, twiddle = [jnp.asarray(t) for t in tables()]
    codes = codes.transpose(1, 2, 0)
    gain_row = gain.reshape(1, CH)
    S = jax.ShapeDtypeStruct
    dma = pltpu.SemaphoreType.DMA
    V = pltpu.VMEM
    given = (field, cot, codes, *tabs, gain_row, inner_w, inner_b, outer_w, twiddle)
    loaded = [V(a.shape, a.dtype) for a in given]
    scratch = loaded + [
        dma((len(loaded),)), V((CH, LON), F32), dma(()),
        V((PT * CH, 2 * QT), BF),
        V((2, CK, NZ, 16, LC), BF), V((2, CK, NZ, 16, LC), BF),
        V((2, CK, NJ, 32, LC), BF), V((2, CK, NJ, 32, LC), BF),
        V((CK, NJ, 32, LC), BF), V((CK, NJ, 32, LC), BF),
        V((CK, NZ, 16, LC), BF), V((CK, NZ, 16, LC), BF),
        V((8, 768), F32), V((4, 8, 768), F32), V((2, 8, 384), F32), V((2, 4, 8, 384), F32),
        V((8, LON), F32), V((CH, 1), F32),
        V((256, 256), BF), V((256, 256), BF), V((8, 256), F32), V((PT, 128, 128), jnp.int32),
        V((PT * 128, 256), BF), V((PT * 128, 256), BF), V((LP, 256), BF), V((LP, 256), BF),
        V((256, LP), BF), V((256, 256), F32), V((256, 256), F32), V((8, 256), F32),
        V((PT * CH, 2 * QT), F32), V((8, LON), F32), V((8, LON), F32),
        V((NJ, RW, 128), F32), V((NJ, RW, 128), F32),
        V((NEAR, 16, 128), F32), V((NEAR, 16, 128), F32), V((16, 128), F32),
        V((NZ // NEAR, 16, 128), F32), V((16, 128), F32), V((NEAR, 16, 128), F32),
        V((RW, 128), F32), V((NJ, RW, 128), F32),
        dma((2, CK)), dma((2, CK)), dma((2, CK)), dma((2, CK)),
        dma((CK,)), dma((CK,)), dma((CK,)), dma((CK,)),
    ] + [dma(()), dma(()), dma((2,)), dma((2,))] + [dma(())] * 10
    grad, cells, weights, small = pl.pallas_call(
        kernel,
        out_shape=(
            S((CH, LON), F32),
            S((8, LON), F32),
            S((4, CH, 128), F32),
            S((8, 128), F32),
        ),
        in_specs=[hbm] * len(given),
        out_specs=(hbm,) + (vm,) * 3,
        scratch_shapes=scratch,
        compiler_params=pltpu.CompilerParams(
            collective_id=0, has_side_effects=True, vmem_limit_bytes=56 * 2**20
        ),
        name="mixing_backward",
    )(*given)
    def fixed(*shape):
        return pl.BlockSpec(shape, lambda i: (0,) * len(shape))

    outs = pl.pallas_call(
        finish,
        out_shape=(
            S((1, CH, LON), BF),
            S((1, 2, CH, CH), F32),
            S((1, 2, CH), F32),
            S((1, 2, CH, CH), F32),
            S((1, 2, CH), F32),
            S((1, CH), F32),
        ),
        grid=(CH // FR,),
        in_specs=[
            pl.BlockSpec((1, FR, LON), lambda i: (0, i, 0)),
            pl.BlockSpec((FR, LON), lambda i: (i, 0)),
            fixed(8, LON),
            fixed(4, CH, 128),
            fixed(8, 128),
        ],
        out_specs=(
            pl.BlockSpec((1, FR, LON), lambda i: (0, i, 0)),
            fixed(1, 2, CH, CH),
            fixed(1, 2, CH),
            fixed(1, 2, CH, CH),
            fixed(1, 2, CH),
            fixed(1, CH),
        ),
        compiler_params=pltpu.CompilerParams(dimension_semantics=("arbitrary",)),
        name="finish",
    )(field, grad, cells, weights, small)
    return outs[:5] + (outs[5].reshape(CH),)


def solution(mesh):
    in_specs = (
        P("lat", "chan", None),
        P("lat", "chan", None),
        P("chan"),
        P("chan", None, None, None),
        P("chan", None, None),
        P("chan", None, None, None),
        P(None, "lat", "chan"),
    )
    out_specs = (
        P("lat", "chan", None),
        P("chan", None, None, None),
        P("chan", None, None),
        P("chan", None, None, None),
        P("chan", None, None),
        P("chan"),
    )
    return jax.shard_map(
        per_device, mesh=mesh, in_specs=in_specs, out_specs=out_specs, check_vma=False
    )
```

```python
import math

import jax
import jax.numpy as jnp
import ml_dtypes
import numpy as np
from jax import lax
from jax.experimental import pallas as pl
from jax.experimental.pallas import tpu as pltpu
from jax.sharding import PartitionSpec as P

MESH = pl.DeviceIdType.MESH
BF = jnp.bfloat16
F32 = jnp.float32

LON = 3072
PT = 12
QT = 256
LAT = 128
CH = 96
ALL_CH = 384
NZ = 16
NJ = 8
CK = 3
MC = PT // CK
LC = MC * CH
LP = MC * 128
RW = 48
FR = 48
NEAR = 4
RP = RW // NEAR


def tables():
    z, p, j = np.meshgrid(np.arange(NZ), np.arange(2), np.arange(NJ), indexing="ij")
    dev = ((j // 4) * 64 + z * 4 + j % 4).reshape(-1)
    part = p.reshape(-1)
    q = np.arange(QT)
    ang = 2 * np.pi * ((dev[:, None] * q[None, :]) % QT) / QT
    cos, sin = np.cos(ang), np.sin(ang)
    re = part[:, None] == 0
    fwd = np.concatenate([np.where(re, cos, -sin), np.where(re, sin, cos)], 1)
    inv = np.concatenate([np.where(re, cos, -sin), np.where(re, sin, cos)], 1)
    j2, p2, z2 = np.meshgrid(np.arange(NJ), np.arange(2), np.arange(NZ), indexing="ij")
    dev2 = ((j2 // 4) * 64 + z2 * 4 + j2 % 4).reshape(-1)
    part2 = p2.reshape(-1)
    mode = np.arange(LAT)
    ang2 = 2 * np.pi * ((mode[:, None] * dev2[None, :]) % LAT) / LAT
    c2, s2 = np.cos(ang2), np.sin(ang2)
    re2 = part2[None, :] == 0
    lat = np.concatenate([np.where(re2, c2, s2), np.where(re2, -s2, c2)], 0) / math.sqrt(LAT)
    pos = (z2 * 2 * NJ + p2 * NJ + j2).reshape(-1)
    perm = np.zeros((256, 256))
    perm[np.arange(256), pos] = 1.0
    widen = np.zeros((LC, LP))
    for i in range(MC):
        widen[i * CH + np.arange(CH), i * 128 + np.arange(CH)] = 1.0
    turn = 2 * np.pi * np.arange(PT)[:, None] * q[None, :] / LON
    twiddle = np.concatenate([np.cos(turn), np.sin(turn)], 0) / math.sqrt(LON)
    order = (fwd, perm @ fwd, inv, lat, lat @ perm, lat.T, perm, perm.T, widen, widen.T)
    bf = [a.astype(ml_dtypes.bfloat16) for a in order]
    return bf + [twiddle.astype(np.float32)]


def real12(u0, u6, s, t):
    h = 0.5
    r3 = math.sqrt(3.0) / 2
    ap, am = u0 + u6, u0 - u6
    s24, d24 = s[2] + s[4], s[2] - s[4]
    s15, d15 = s[1] + s[5], s[1] - s[5]
    e0, o0 = ap + s24, s15 + s[3]
    e1, o1 = am + h * d24, r3 * d15
    e2, o2 = ap - h * s24, h * s15 - s[3]
    real = [e0 + o0, e1 + o1, e2 + o2, am - d24, e2 - o2, e1 - o1, e0 - o0]
    t15, f15 = t[1] + t[5], t[1] - t[5]
    t24, f24 = t[2] + t[4], t[2] - t[4]
    a1, b1 = h * t15 + t[3], r3 * t24
    a2, b2 = r3 * f15, r3 * f24
    imag = [None, -(a1 + b1), -(a2 + b2), t[3] - t15, b2 - a2, b1 - a1, None]
    return real, imag


def dot_nn(a, b):
    return lax.dot_general(a, b, (((1,), (0,)), ((), ())), preferred_element_type=F32)


def dot_nt(a, b):
    return lax.dot_general(a, b, (((1,), (1,)), ((), ())), preferred_element_type=F32)


def dot_tn(a, b):
    return lax.dot_general(a, b, (((0,), (0,)), ((), ())), preferred_element_type=F32)


def kernel(
    x_hbm, cot_hbm, code_hbm, fwd_hbm, fwdx_hbm, inv_hbm, lat_hbm, latz_hbm, lati_hbm,
    perm_hbm, permi_hbm, wide_hbm, narrow_hbm,
    gain_hbm, iw_hbm, ib_hbm, ow_hbm, tw_hbm,
    g_hbm, cell_ref, wout_ref, bout_ref,
    x_ref, cot_ref, code_ref, fwd_ref, fwdx_ref, inv_ref, lat_ref, latz_ref, lati_ref,
    perm_ref, permi_ref, wide_ref, narrow_ref, gain_ref, iw_ref, ib_ref, ow_ref, tw_ref,
    load_sem, g_ref, g_sem,
    ybuf, zs, zr, xs, xr, bxs, bxr, bzs, bzr,
    stat_s, stat_r, tail_s, tail_r, mr, gcol,
    m1, m2, bias, cm, sg_all, bh_all, fi, hd, gp, p1, p2, bsum,
    vbuf, hacc, cacc,
    rw, rr1, rs, rr2, rt, rr3, ru, rr4, rv, rr5,
    zs_sem, zr_sem, xs_sem, xr_sem, bxs_sem, bxr_sem, bzs_sem, bzr_sem,
    st_ssem, st_rsem, tl_ssem, tl_rsem,
    r1_ssem, r1_rsem, r2_ssem, r2_rsem, r3_ssem, r3_rsem, r4_ssem, r4_rsem, r5_ssem, r5_rsem,
):
    me = lax.axis_index("lat")
    chan = lax.axis_index("chan")
    x = me // 64
    z = lax.rem(me // 4, NZ)
    y = lax.rem(me, 4)
    j = x * 4 + y
    base_z = me - z * 4

    def z_step(t):
        half = t // 2
        odd = lax.rem(t, 2)
        off = (half + 1) * (1 - odd) + (NZ - 1 - half) * odd
        to = lax.rem(z + off, NZ)
        return to, {"lat": base_z + to * 4}

    def xy_step(t):
        d = t + 1
        tx = lax.rem(x + d // 4, 2)
        ty = lax.rem(y + lax.rem(d, 4), 4)
        return tx * 4 + ty, {"lat": tx * 64 + z * 4 + ty}

    near, block = lax.rem(z, NEAR), z // NEAR

    def near_step(t):
        to = lax.rem(near + t + 1, NEAR)
        return to, {"lat": base_z + (block * NEAR + to) * 4}

    def far_step(t):
        to = lax.rem(block + t + 1, NZ // NEAR)
        return to, {"lat": base_z + (to * NEAR + near) * 4}

    def chan_step(t):
        to = lax.rem(chan + t + 1, 4)
        return to, {"chan": to}

    def each(count, body):
        def one(t, carry):
            body(t)
            return carry

        lax.fori_loop(0, count, one, 0)

    def remote(src, dst, ssem, rsem, to):
        pltpu.make_async_remote_copy(
            src_ref=src, dst_ref=dst, send_sem=ssem, recv_sem=rsem, device_id=to, device_id_type=MESH
        ).start()

    def drain(ref, sem):
        pltpu.make_async_copy(ref, ref, sem).wait()

    def z_exchange(src, dst, ssem, rsem):
        def send(t):
            to, dev = z_step(t)
            remote(src.at[to], dst.at[z], ssem, rsem, dev)

        each(NZ - 1, send)
        dst[z] = src[z]

    def xy_exchange(src, dst, ssem, rsem):
        def send(t):
            to, dev = xy_step(t)
            remote(src.at[to], dst.at[j], ssem, rsem, dev)

        each(NJ - 1, send)
        dst[j] = src[j]

    def share(step, count, place, src, dst, ssem, rsem):
        def send(t):
            _, dev = step(t)
            remote(src, dst.at[place], ssem, rsem, dev)

        each(count - 1, send)
        dst[place] = src[...]

    def chan_share(src, dst, ssem, rsem):
        share(chan_step, 4, chan, src, dst, ssem, rsem)

    def rest(ref, count, sem):
        drain(ref.at[pl.ds(0, count - 1)], sem)

    def z_done(ref, sem):
        drain(ref.at[pl.ds(0, NZ - 1)], sem)

    def xy_done(ref, sem):
        drain(ref.at[pl.ds(0, NJ - 1)], sem)

    barrier = pltpu.get_barrier_semaphore()

    def greet(step):
        def one(t):
            _, dev = step(t)
            pl.semaphore_signal(barrier, inc=1, device_id=dev, device_id_type=MESH)

        return one

    each(NZ - 1, greet(lambda t: z_step(NZ - 2 - t)))
    each(NJ - 1, greet(xy_step))
    each(3, greet(chan_step))

    loads = [
        pltpu.make_async_copy(src, dst, load_sem.at[k])
        for k, (src, dst) in enumerate((
            (cot_hbm, cot_ref), (fwd_hbm, fwd_ref), (x_hbm, x_ref), (fwdx_hbm, fwdx_ref),
            (permi_hbm, permi_ref), (perm_hbm, perm_ref), (code_hbm, code_ref), (wide_hbm, wide_ref),
            (lat_hbm, lat_ref), (lati_hbm, lati_ref), (narrow_hbm, narrow_ref),
            (latz_hbm, latz_ref), (inv_hbm, inv_ref), (gain_hbm, gain_ref), (iw_hbm, iw_ref),
            (ib_hbm, ib_ref), (ow_hbm, ow_ref), (tw_hbm, tw_ref),
        ))
    ]
    for load in (loads[17], *loads[:17]):
        load.start()
    loads[17].wait()
    loads[0].wait()

    def lanes(p):
        return slice(p * QT, (p + 1) * QT)

    def forward_rows(load):
        def block(r):
            r0 = pl.multiple_of(r * 16, 16)
            u = [load(r0, p) for p in range(PT)]
            s = [None] + [u[p] + u[PT - p] for p in range(1, 6)]
            t = [None] + [u[p] - u[PT - p] for p in range(1, 6)]
            real, imag = real12(u[0], u[6], s, t)
            for i in range(PT):
                k = i if i <= 6 else PT - i
                yr = real[k]
                yi = imag[k]
                c = tw_ref[i : i + 1, :]
                w = tw_ref[PT + i : PT + i + 1, :]
                if yi is None:
                    ar, ai = yr * c, -(yr * w)
                elif i <= 6:
                    ar, ai = yr * c + yi * w, yi * c - yr * w
                else:
                    ar, ai = yr * c - yi * w, -(yi * c) - yr * w
                rows = pl.ds(pl.multiple_of(i * CH + r0, 16), 16)
                ybuf[rows, 0:QT] = ar.astype(BF)
                ybuf[rows, QT : 2 * QT] = ai.astype(BF)

        each(CH // 16, block)

    def dft_chunk(table, c):
        return dot_nt(table[...], ybuf[pl.ds(c * LC, LC), :])

    forward_rows(lambda r0, p: cot_ref[0, pl.ds(r0, 16), lanes(p)].astype(F32))
    loads[1].wait()
    for c in range(CK):
        out = dft_chunk(fwd_ref, c)
        if c == 0:
            row = lax.broadcasted_iota(jnp.int32, out.shape, 0)
            lane = lax.broadcasted_iota(jnp.int32, out.shape, 1)
            first = ((row == 0) | (row == NJ)) & (lane < CH)
            out = out * jnp.where(first, 0.5, 1.0)
        zs[0, c] = out.astype(BF).reshape(NZ, 16, LC)
        if c == 0:
            pl.semaphore_wait(barrier, NZ - 1 + NJ - 1 + 3)
        z_exchange(zs.at[0, c], zr.at[0, c], zs_sem.at[0, c], zr_sem.at[0, c])

    loads[2].wait()
    for p in range(PT):
        v = x_ref[0, :, lanes(p)].astype(F32)
        total = jnp.sum(v, axis=0, keepdims=True)
        off = v - total * (1.0 / CH)
        r, l = p // 3, (p % 3) * QT
        stat_s[r : r + 1, l : l + QT] = total
        stat_s[4 + r : 5 + r, l : l + QT] = jnp.sum(off * off, axis=0, keepdims=True)
    chan_share(stat_s, stat_r, st_ssem, st_rsem)

    for k in (13, 14, 15, 16):
        loads[k].wait()
    diag = (
        lax.broadcasted_iota(jnp.int32, (CH, CH), 0) == lax.broadcasted_iota(jnp.int32, (CH, CH), 1)
    ).astype(F32)
    gcol[...] = jnp.sum(diag * gain_ref[...], axis=1, keepdims=True)
    for m, w in ((m1, iw_ref), (m2, ow_ref)):
        m[...] = jnp.zeros(m.shape, BF)
        m[0:CH, 0:CH] = w[0, 0]
        m[0:CH, 128 : 128 + CH] = w[0, 1]
        m[128 : 128 + CH, 0:CH] = -w[0, 1]
        m[128 : 128 + CH, 128 : 128 + CH] = w[0, 0]
    bias[...] = jnp.zeros(bias.shape, F32)
    bias[0:1, 0:CH] = ib_ref[0, 0:1, :]
    bias[0:1, 128 : 128 + CH] = ib_ref[0, 1:2, :]
    cm[...] = jnp.zeros(cm.shape, jnp.int32)
    loads[6].wait()
    for i in range(PT):
        cm[i, :, 0:CH] = code_ref[i].T
    p1[...] = jnp.zeros(p1.shape, F32)
    p2[...] = jnp.zeros(p2.shape, F32)
    bsum[...] = jnp.zeros(bsum.shape, F32)

    drain(stat_r.at[pl.ds(0, 3)], st_rsem)
    for p in range(PT):
        r, l = p // 3, (p % 3) * QT
        sums = [stat_r[d, r : r + 1, l : l + QT] for d in range(4)]
        spreads = [stat_r[d, 4 + r : 5 + r, l : l + QT] for d in range(4)]
        mean = (sums[0] + sums[1] + sums[2] + sums[3]) * (1.0 / ALL_CH)
        spread = spreads[0] + spreads[1] + spreads[2] + spreads[3]
        for d in range(4):
            gap = sums[d] * (1.0 / CH) - mean
            spread = spread + CH * gap * gap
        mr[0:1, lanes(p)] = mean
        mr[1:2, lanes(p)] = lax.rsqrt(spread * (1.0 / ALL_CH) + 1e-05)

    def xhat(r0, p):
        v = x_ref[0, pl.ds(r0, 16), lanes(p)].astype(F32)
        return (v - mr[0:1, lanes(p)]) * mr[1:2, lanes(p)]

    forward_rows(lambda r0, p: xhat(r0, p) * gcol[pl.ds(r0, 16), :])
    for k in (3, 4, 5):
        loads[k].wait()
    for c in range(CK):
        xs[1, c] = dft_chunk(fwdx_ref, c).astype(BF).reshape(NJ, 32, LC)
        xy_exchange(xs.at[1, c], xr.at[1, c], xs_sem.at[1, c], xr_sem.at[1, c])

    def ready_input(c):
        xy_done(xr.at[1, c], xr_sem.at[1, c])
        got = xr[1, c].reshape(256, LC)
        zs[1, c] = dot_nn(permi_ref[...], got).astype(BF).reshape(NZ, 16, LC)

    def send_input(c):
        z_exchange(zs.at[1, c], zr.at[1, c], zs_sem.at[1, c], zr_sem.at[1, c])

    def second_exchange(c):
        z_done(zr.at[0, c], zr_sem.at[0, c])
        got = zr[0, c].reshape(256, LC)
        xs[0, c] = dot_nn(perm_ref[...], got).astype(BF).reshape(NJ, 32, LC)
        xy_exchange(xs.at[0, c], xr.at[0, c], xs_sem.at[0, c], xr_sem.at[0, c])

    def latitude_modes(table, pencil):
        spread = dot_nn(pencil.reshape(256, LC), wide_ref[...]).astype(BF)
        return dot_nn(table[...], spread)

    def bit(code, place):
        if place >= 2:
            return jnp.bitwise_and(jnp.right_shift(code, place - 1), 2).astype(F32)
        return jnp.bitwise_and(jnp.right_shift(code, place), 1).astype(F32)

    def mode_rows(c, i):
        return slice((c * MC + i) * 128, (c * MC + i + 1) * 128)

    def masked(dst, rows, value, code, place):
        dst[rows, 0:128] = (value[0] * bit(code, place)).astype(BF)
        dst[rows, 128:256] = (value[1] * bit(code, place + 1)).astype(BF)

    def backward_chunk(c):
        xy_done(xr.at[0, c], xr_sem.at[0, c])
        freq = latitude_modes(lat_ref, xr[0, c])
        for i in range(MC):
            col = slice(i * 128, (i + 1) * 128)
            masked(sg_all, mode_rows(c, i), (freq[0:128, col], freq[128:256, col]), cm[c * MC + i], 2)
        chunk = slice(c * LP, (c + 1) * LP)
        back = dot_nt(sg_all[chunk, :], m2[...])
        for i in range(MC):
            row = slice(i * 128, (i + 1) * 128)
            masked(bh_all, mode_rows(c, i), (back[row, 0:128], back[row, 128:256]), cm[c * MC + i], 0)
        grad = dot_nt(bh_all[chunk, :], m1[...]).astype(BF)
        for i in range(MC):
            row = slice(i * 128, (i + 1) * 128)
            gp[0:128, row] = grad[row, 0:128]
            gp[128:256, row] = grad[row, 128:256]
        spec = dot_nn(lati_ref[...], gp[...]).astype(BF)
        bxs[c] = dot_nn(spec, narrow_ref[...]).astype(BF).reshape(NJ, 32, LC)
        xy_exchange(bxs.at[c], bxr.at[c], bxs_sem.at[c], bxr_sem.at[c])
        bsum[0:1, :] += jnp.sum(bh_all[chunk, :].astype(F32), axis=0, keepdims=True)
        bsum[1:2, :] += jnp.sum(sg_all[chunk, :].astype(F32), axis=0, keepdims=True)

    def second_back(c):
        xy_done(bxr.at[c], bxr_sem.at[c])
        got = bxr[c].reshape(256, LC)
        bzs[c] = dot_nn(permi_ref[...], got).astype(BF).reshape(NZ, 16, LC)

    def send_back(c):
        z_exchange(bzs.at[c], bzr.at[c], bzs_sem.at[c], bzr_sem.at[c])

    def sum_parts(s, src):
        real = src[0:CH, 0:128] + src[128 : 128 + CH, 128:256]
        imag = src[0:CH, 128:256] - src[128 : 128 + CH, 0:128]
        rw[s, 0:48] = real[0:48]
        rw[s + 1, 0:48] = real[48:96]
        rw[s + 2, 0:48] = imag[0:48]
        rw[s + 3, 0:48] = imag[48:96]

    def send_parts(outer):
        def send(t):
            to, dev = xy_step(t)

            @pl.when((to >= 4) if outer else (to < 4))
            def _():
                remote(rw.at[to], rr1.at[j], r1_ssem, r1_rsem, dev)

        each(NJ - 1, send)

    def weight_chunk(c):
        z_done(zr.at[1, c], zr_sem.at[1, c])
        if c == CK - 1:
            send_back(1)
        freq = latitude_modes(latz_ref, zr[1, c])
        for i in range(MC):
            row = slice(i * 128, (i + 1) * 128)
            fi[row, 0:128] = freq[0:128, row].astype(BF)
            fi[row, 128:256] = freq[128:256, row].astype(BF)
        pre = dot_nn(fi[...], m1[...]) + bias[0:1, :]
        for i in range(MC):
            row = slice(i * 128, (i + 1) * 128)
            masked(hd, row, (pre[row, 0:128], pre[row, 128:256]), cm[c * MC + i], 0)
        chunk = slice(c * LP, (c + 1) * LP)
        sg, bh = sg_all[chunk, :], bh_all[chunk, :]
        p2[...] += dot_tn(hd[...], sg)
        if c == CK - 1:
            sum_parts(4, p2)
            send_parts(True)
        p1[...] += dot_tn(fi[...], bh)

    for c in range(CK):
        ready_input(c)
    second_exchange(0)
    send_input(0)
    second_exchange(1)
    send_input(1)
    for k in (7, 8, 9, 10):
        loads[k].wait()
    backward_chunk(0)
    second_exchange(2)
    send_input(2)
    backward_chunk(1)
    second_back(0)
    backward_chunk(2)
    second_back(1)
    loads[11].wait()
    weight_chunk(0)
    send_back(0)
    second_back(2)
    weight_chunk(1)
    weight_chunk(2)

    sum_parts(0, p1)
    for r in range(4):
        for k in range(3):
            l = (r % 2) * 128 + 32 * k
            rw[0, 3 * r + k : 3 * r + k + 1, CH:128] = bsum[r // 2 : r // 2 + 1, l : l + 32]
    send_parts(False)
    rr1[j] = rw[j]

    def inverse_chunk(c):
        z_done(bzr.at[c], bzr_sem.at[c])
        got = bzr[c].reshape(256, LC)
        out = dot_tn(got, inv_ref[...])
        for k in range(MC):
            i = c * MC + k
            vr = out[k * CH : (k + 1) * CH, 0:QT]
            vi = out[k * CH : (k + 1) * CH, QT : 2 * QT]
            co = tw_ref[i : i + 1, :]
            si = tw_ref[PT + i : PT + i + 1, :]
            vbuf[i * CH : (i + 1) * CH, 0:QT] = vr * co - vi * si
            if i not in (0, 6):
                vbuf[i * CH : (i + 1) * CH, QT : 2 * QT] = vr * si + vi * co

    loads[12].wait()

    def total(ref, count):
        part = ref[0]
        for s in range(1, count):
            part = part + ref[s]
        return part

    xy_done(rr1, r1_rsem)
    part = total(rr1, NJ)
    rs[...] = jnp.zeros(rs.shape, F32)
    for k in range(NEAR):
        rs[k, 0:RP] = part[k * RP : (k + 1) * RP]

    def send_near(t):
        to, dev = near_step(t)
        remote(rs.at[to], rr2.at[near], r2_ssem, r2_rsem, dev)

    each(NEAR - 1, send_near)
    rr2[near] = rs[near]
    rest(rr2, NEAR, r2_rsem)
    rt[...] = total(rr2, NEAR)
    share(far_step, NZ // NEAR, block, rt, rr3, r3_ssem, r3_rsem)
    send_back(2)
    inverse_chunk(0)
    inverse_chunk(1)
    rest(rr3, NZ // NEAR, r3_rsem)
    ru[...] = total(rr3, NZ // NEAR)
    share(near_step, NEAR, near, ru, rr4, r4_ssem, r4_rsem)
    rest(rr4, NEAR, r4_rsem)
    for k in range(NEAR):
        rv[k * RP : (k + 1) * RP] = rr4[k, 0:RP]
    share(xy_step, NJ, j, rv, rr5, r5_ssem, r5_rsem)
    inverse_chunk(2)

    hacc[...] = jnp.zeros(hacc.shape, F32)
    cacc[...] = jnp.zeros(cacc.shape, F32)

    half_lanes = [[slice(p * QT + h * 128, p * QT + h * 128 + 128) for p in range(PT)] for h in range(2)]

    for h in range(2):
        at = half_lanes[h]

        def inverse_rows(r):
            r0 = pl.multiple_of(r * 32, 32)
            re, im = [], []
            for i in range(PT):
                rows = pl.ds(pl.multiple_of(i * CH + r0, 32), 32)
                re.append(vbuf[rows, h * 128 : h * 128 + 128])
                im.append(None if i in (0, 6) else vbuf[rows, QT + h * 128 : QT + h * 128 + 128])
            s = [None] + [re[i] + re[PT - i] for i in range(1, 6)]
            t = [None] + [im[i] - im[PT - i] for i in range(1, 6)]
            real, imag = real12(re[0], re[6], s, t)
            column = gcol[pl.ds(r0, 32), :]
            for p in range(PT):
                k = p if p <= 6 else PT - p
                v = real[k]
                if imag[k] is not None:
                    v = v + imag[k] if p <= 6 else v - imag[k]
                v = v * column
                g_ref[pl.ds(r0, 32), at[p]] = v
                field = x_ref[0, pl.ds(r0, 32), at[p]].astype(F32)
                w = v * ((field - mr[0:1, at[p]]) * mr[1:2, at[p]])
                hacc[:, at[p]] += (v[0:8] + v[8:16]) + (v[16:24] + v[24:32])
                cacc[:, at[p]] += (w[0:8] + w[8:16]) + (w[16:24] + w[24:32])

        each(CH // 32, inverse_rows)
        for p in range(PT):
            r, l = p // 3, (p % 3) * 128
            tail_s[h, r : r + 1, l : l + 128] = jnp.sum(hacc[:, at[p]], axis=0, keepdims=True)
            tail_s[h, 4 + r : 5 + r, l : l + 128] = jnp.sum(cacc[:, at[p]], axis=0, keepdims=True)
        chan_share(tail_s.at[h], tail_r.at[h], tl_ssem.at[h], tl_rsem.at[h])

    g_copy = pltpu.make_async_copy(g_ref, g_hbm, g_sem)
    g_copy.start()

    xy_done(rr5, r5_rsem)
    scale = 1.0 / math.sqrt(LAT * LON / 2)
    for s in range(4):
        for k in range(2):
            wout_ref[s, k * 48 : (k + 1) * 48] = rr5[2 * s + k, 0:48] * scale
    for r in range(4):
        for k in range(3):
            row = rr5[0, 3 * r + k : 3 * r + k + 1, CH:128]
            bout_ref[r : r + 1, 32 * k : 32 * k + 32] = row * scale
    product = jnp.zeros((CH, CH), F32)
    for k in range(2):
        product = product + wout_ref[k, :, 0:CH] * iw_ref[0, k].astype(F32)
    column = jnp.sum(product, axis=1, keepdims=True)
    as_row = jnp.sum(diag * column, axis=0, keepdims=True)
    bout_ref[4:5, 0:CH] = as_row * (1.0 / math.sqrt(LAT * LON) / scale) / gain_ref[...]

    for h in range(2):
        drain(tail_r.at[h, pl.ds(0, 3)], tl_rsem.at[h])
        for p in range(PT):
            r, l = p // 3, (p % 3) * 128
            for k in range(2):
                q = 4 * k + r
                whole = tail_r[h, 0, q : q + 1, l : l + 128]
                for d in range(1, 4):
                    whole = whole + tail_r[h, d, q : q + 1, l : l + 128]
                mr[2 + k : 3 + k, half_lanes[h][p]] = whole * (1.0 / ALL_CH)
    cell_ref[...] = mr[...]

    g_copy.wait()
    for c in range(CK):
        for f in range(2):
            z_done(zs.at[f, c], zs_sem.at[f, c])
            xy_done(xs.at[f, c], xs_sem.at[f, c])
        xy_done(bxs.at[c], bxs_sem.at[c])
        z_done(bzs.at[c], bzs_sem.at[c])
    drain(stat_r.at[pl.ds(0, 3)], st_ssem)
    for h in range(2):
        drain(tail_r.at[h, pl.ds(0, 3)], tl_ssem.at[h])
    xy_done(rw, r1_ssem)
    rest(rr2, NEAR, r2_ssem)
    rest(rr3, NZ // NEAR, r3_ssem)
    rest(rr4, NEAR, r4_ssem)
    xy_done(rr5, r5_ssem)


def finish(
    x_ref, g_ref, cell_ref, w_ref, b_ref, gin_ref, giw_ref, gib_ref, gow_ref, gob_ref, gg_ref
):
    mean, rstd = cell_ref[0:1, :], cell_ref[1:2, :]
    normed = (x_ref[0].astype(F32) - mean) * rstd
    value = g_ref[...] - cell_ref[2:3, :] - normed * cell_ref[3:4, :]
    gin_ref[0] = (value * rstd).astype(BF)

    @pl.when(pl.program_id(0) == 0)
    def _():
        for k in range(2):
            giw_ref[0, k] = w_ref[k, :, 0:CH]
            gow_ref[0, k] = w_ref[2 + k, :, 0:CH]
        gib_ref[0] = b_ref[0:2, 0:CH]
        gob_ref[0] = b_ref[2:4, 0:CH]
        gg_ref[...] = b_ref[4:5, 0:CH]


def per_device(field, cot, gain, inner_w, inner_b, outer_w, codes):
    vm = pl.BlockSpec(memory_space=pltpu.VMEM)
    hbm = pl.BlockSpec(memory_space=pl.ANY)
    *tabs, twiddle = [jnp.asarray(t) for t in tables()]
    codes = codes.transpose(1, 2, 0)
    gain_row = gain.reshape(1, CH)
    S = jax.ShapeDtypeStruct
    dma = pltpu.SemaphoreType.DMA
    V = pltpu.VMEM
    given = (field, cot, codes, *tabs, gain_row, inner_w, inner_b, outer_w, twiddle)
    loaded = [V(a.shape, a.dtype) for a in given]
    scratch = loaded + [
        dma((len(loaded),)), V((CH, LON), F32), dma(()),
        V((PT * CH, 2 * QT), BF),
        V((2, CK, NZ, 16, LC), BF), V((2, CK, NZ, 16, LC), BF),
        V((2, CK, NJ, 32, LC), BF), V((2, CK, NJ, 32, LC), BF),
        V((CK, NJ, 32, LC), BF), V((CK, NJ, 32, LC), BF),
        V((CK, NZ, 16, LC), BF), V((CK, NZ, 16, LC), BF),
        V((8, 768), F32), V((4, 8, 768), F32), V((2, 8, 384), F32), V((2, 4, 8, 384), F32),
        V((8, LON), F32), V((CH, 1), F32),
        V((256, 256), BF), V((256, 256), BF), V((8, 256), F32), V((PT, 128, 128), jnp.int32),
        V((PT * 128, 256), BF), V((PT * 128, 256), BF), V((LP, 256), BF), V((LP, 256), BF),
        V((256, LP), BF), V((256, 256), F32), V((256, 256), F32), V((8, 256), F32),
        V((PT * CH, 2 * QT), F32), V((8, LON), F32), V((8, LON), F32),
        V((NJ, RW, 128), F32), V((NJ, RW, 128), F32),
        V((NEAR, 16, 128), F32), V((NEAR, 16, 128), F32), V((16, 128), F32),
        V((NZ // NEAR, 16, 128), F32), V((16, 128), F32), V((NEAR, 16, 128), F32),
        V((RW, 128), F32), V((NJ, RW, 128), F32),
        dma((2, CK)), dma((2, CK)), dma((2, CK)), dma((2, CK)),
        dma((CK,)), dma((CK,)), dma((CK,)), dma((CK,)),
    ] + [dma(()), dma(()), dma((2,)), dma((2,))] + [dma(())] * 10
    grad, cells, weights, small = pl.pallas_call(
        kernel,
        out_shape=(
            S((CH, LON), F32),
            S((8, LON), F32),
            S((4, CH, 128), F32),
            S((8, 128), F32),
        ),
        in_specs=[hbm] * len(given),
        out_specs=(hbm,) + (vm,) * 3,
        scratch_shapes=scratch,
        compiler_params=pltpu.CompilerParams(
            collective_id=0, has_side_effects=True, vmem_limit_bytes=56 * 2**20
        ),
        name="mixing_backward",
    )(*given)
    def fixed(*shape):
        return pl.BlockSpec(shape, lambda i: (0,) * len(shape))

    outs = pl.pallas_call(
        finish,
        out_shape=(
            S((1, CH, LON), BF),
            S((1, 2, CH, CH), F32),
            S((1, 2, CH), F32),
            S((1, 2, CH, CH), F32),
            S((1, 2, CH), F32),
            S((1, CH), F32),
        ),
        grid=(CH // FR,),
        in_specs=[
            pl.BlockSpec((1, FR, LON), lambda i: (0, i, 0)),
            pl.BlockSpec((FR, LON), lambda i: (i, 0)),
            fixed(8, LON),
            fixed(4, CH, 128),
            fixed(8, 128),
        ],
        out_specs=(
            pl.BlockSpec((1, FR, LON), lambda i: (0, i, 0)),
            fixed(1, 2, CH, CH),
            fixed(1, 2, CH),
            fixed(1, 2, CH, CH),
            fixed(1, 2, CH),
            fixed(1, CH),
        ),
        compiler_params=pltpu.CompilerParams(dimension_semantics=("arbitrary",)),
        name="finish",
    )(field, grad, cells, weights, small)
    return outs[:5] + (outs[5].reshape(CH),)


def solution(mesh):
    in_specs = (
        P("lat", "chan", None),
        P("lat", "chan", None),
        P("chan"),
        P("chan", None, None, None),
        P("chan", None, None),
        P("chan", None, None, None),
        P(None, "lat", "chan"),
    )
    out_specs = (
        P("lat", "chan", None),
        P("chan", None, None, None),
        P("chan", None, None),
        P("chan", None, None, None),
        P("chan", None, None),
        P("chan"),
    )
    return jax.shard_map(
        per_device, mesh=mesh, in_specs=in_specs, out_specs=out_specs, check_vma=False
    )
```
